32 devices in a mesh: dp: 4 (over x, core), gx: 2 (over y), gy: 4 (over z).
Axes of the slice: x: 2, y: 2, z: 4, core: 2. Of those that a mesh axis runs over, the one named last changes fastest.
Arguments:
- field: bfloat16 [4, 32, 128, 128, 128], P('dp', None, 'gx', 'gy'), may hold values from -6 to 6
- cotangent: bfloat16 [4, 32, 128, 128, 128], P('dp', None, 'gx', 'gy'), may hold values from -6 to 6
- spectral_weight: float32 [16, 32, 16, 2, 1024], P('gy', 'gx'), may hold values from -8 to 8
Outputs:
- field_out: bfloat16 [4, 32, 128, 128, 128], P('dp', None, 'gx', 'gy')
- grad_field: bfloat16 [4, 32, 128, 128, 128], P('dp', None, 'gx', 'gy')
- weight_grad: float32 [16, 32, 16, 2, 1024], P('gy', 'gx', 'dp')
The draws below stay inside these ranges and needn't reach their ends.
All inputs are finite; a program needn't handle non-finite values.
Results may differ from the reference program's by a relative error of at most 0.0057.
Values may be sent and summed in bfloat16 or wider, within the bound.
No kernel may reach another device: no remote copies, remote signals or barrier semaphores. Data moves between devices by JAX's collectives and lax.ppermute only.
A program may use at most 320 MiB of HBM per device.

```python
import math
import jax
import jax.numpy as jnp
from jax import lax

CHANNELS = 32
NX = 128
NY = 128
NZ = 128
MX = 16
MY = 16
MZ = 32
SAMPLES = 4


def steps_of(rng, extent, shards, smallest, top_value):
    loudness, own = 1.0, jax.random.fold_in(rng, 6)
    for axis_at, blocks in shards:
        steps = jnp.exp(jax.random.uniform(jax.random.fold_in(own, axis_at), (blocks,), jnp.float32, smallest / len(shards), top_value / len(shards)))
        loudness = loudness * jnp.repeat(steps, extent[axis_at] // blocks).reshape([-1 if axis == axis_at else 1 for axis in range(len(extent))])
    return loudness


def gaussian(own_key, dims, spread, bound, pieces=(), held_as=jnp.bfloat16):
    array = spread * jax.random.normal(own_key, dims, jnp.float32)
    if pieces:
        array = array * steps_of(own_key, dims, pieces, -0.22, 0.18)
    return jnp.clip(array, -bound, bound).astype(held_as)


def setup_inputs(seed: int = 0) -> dict:
    key_list = jax.random.split(jax.random.key(seed), 4)
    field = gaussian(key_list[0], (SAMPLES, CHANNELS, NX, NY, NZ), 1.0, 6.0, ((0, 4), (2, 2), (3, 4)))
    cotangent = gaussian(key_list[1], (SAMPLES, CHANNELS, NX, NY, NZ), 1.0, 6.0, ((0, 4), (2, 2), (3, 4)))
    spectral_weight = gaussian(key_list[2], (MX, MZ, MY, 2, CHANNELS * CHANNELS), 1.4, 8.0, ((0, 4), (1, 2)), jnp.float32)
    return dict(field=field, cotangent=cotangent, spectral_weight=spectral_weight)


PRECISE = lax.Precision.HIGHEST


def mode_list(length, count):
    half_ids = jnp.arange(count // 2, dtype=jnp.int32)
    return jnp.concatenate([half_ids, length - count // 2 + half_ids])


def phase_tables(length, mode_ids):
    cell_ids = jnp.arange(length, dtype=jnp.int32)
    turn_ids = (cell_ids[:, None] * mode_ids[None, :]) % length
    angles = turn_ids.astype(jnp.float32) * (2.0 * math.pi / length)
    return jnp.cos(angles), jnp.sin(angles)


def depth_scales():
    mode_ids = jnp.arange(MZ, dtype=jnp.int32)
    return jnp.where(mode_ids == 0, 1.0, 2.0).astype(jnp.float32) / float(NX * NY * NZ)


def depth_forward(scale_vec):
    cosine, sine_tab = phase_tables(NZ, jnp.arange(MZ, dtype=jnp.int32))
    table_in = jnp.stack([cosine, -sine_tab], axis=2) * scale_vec[None, :, None]
    return table_in.astype(jnp.bfloat16)


def depth_inverse(scale_vec):
    cosine, sine_tab = phase_tables(NZ, jnp.arange(MZ, dtype=jnp.int32))
    return jnp.stack([cosine.T, -sine_tab.T], axis=1) * scale_vec[:, None, None]


def spectral_lead(data_in, length, count):
    cosine, sine_tab = phase_tables(length, mode_list(length, count))
    part_c = jnp.einsum('lkpr,lm->mkpr', data_in, cosine, precision=PRECISE)
    part_s = jnp.einsum('lkpr,lm->mkpr', data_in, sine_tab, precision=PRECISE)
    real_part = part_c[:, :, 0] + part_s[:, :, 1]
    imag_part = part_c[:, :, 1] - part_s[:, :, 0]
    return jnp.stack([real_part, imag_part], axis=2)


def synthesis_lead(data_in, length, count):
    cosine, sine_tab = phase_tables(length, mode_list(length, count))
    part_c = jnp.einsum('mkpr,lm->lkpr', data_in, cosine, precision=PRECISE)
    part_s = jnp.einsum('mkpr,lm->lkpr', data_in, sine_tab, precision=PRECISE)
    real_part = part_c[:, :, 0] - part_s[:, :, 1]
    imag_part = part_s[:, :, 0] + part_c[:, :, 1]
    return jnp.stack([real_part, imag_part], axis=2)


def spectral_rows(data_in, length, count):
    cosine, sine_tab = phase_tables(length, mode_list(length, count))
    part_c = jnp.einsum('akplc,lm->akpmc', data_in, cosine, precision=PRECISE)
    part_s = jnp.einsum('akplc,lm->akpmc', data_in, sine_tab, precision=PRECISE)
    real_part = part_c[:, :, 0] + part_s[:, :, 1]
    imag_part = part_c[:, :, 1] - part_s[:, :, 0]
    return jnp.stack([real_part, imag_part], axis=2)


def synthesis_rows(data_in, length, count):
    cosine, sine_tab = phase_tables(length, mode_list(length, count))
    part_c = jnp.einsum('akpmc,lm->akplc', data_in, cosine, precision=PRECISE)
    part_s = jnp.einsum('akpmc,lm->akplc', data_in, sine_tab, precision=PRECISE)
    real_part = part_c[:, :, 0] - part_s[:, :, 1]
    imag_part = part_s[:, :, 0] + part_c[:, :, 1]
    return jnp.stack([real_part, imag_part], axis=2)


def channel_product(left_op, right_op):
    return jnp.einsum('akjc,akjco->akjo', left_op, right_op, precision=PRECISE)


def channel_adjoint(left_op, right_op):
    return jnp.einsum('akjo,akjco->akjc', left_op, right_op, precision=PRECISE)


def outer_sum(left_op, right_op):
    return jnp.einsum('akjc,akjo->akjco', left_op, right_op, precision=PRECISE)


def mix_modes(spectrum, weight):
    real_in, imag_in = spectrum[:, :, 0], spectrum[:, :, 1]
    w_real, w_imag = weight[:, :, :, 0], weight[:, :, :, 1]
    real_part = channel_product(real_in, w_real) - channel_product(imag_in, w_imag)
    imag_part = channel_product(imag_in, w_real) + channel_product(real_in, w_imag)
    return jnp.stack([real_part, imag_part], axis=2)


def mix_adjoint(spectrum, weight):
    real_in, imag_in = spectrum[:, :, 0], spectrum[:, :, 1]
    w_real, w_imag = weight[:, :, :, 0], weight[:, :, :, 1]
    real_part = channel_adjoint(real_in, w_real) + channel_adjoint(imag_in, w_imag)
    imag_part = channel_adjoint(imag_in, w_real) - channel_adjoint(real_in, w_imag)
    return jnp.stack([real_part, imag_part], axis=2)


def weight_terms(spec_u, spec_g):
    u_real, u_imag = spec_u[:, :, 0], spec_u[:, :, 1]
    g_real, g_imag = spec_g[:, :, 0], spec_g[:, :, 1]
    real_part = outer_sum(u_real, g_real) + outer_sum(u_imag, g_imag)
    imag_part = outer_sum(u_real, g_imag) - outer_sum(u_imag, g_real)
    stacked = jnp.stack([real_part, imag_part], axis=3)
    lead_len, mode_len, row_len, chan_len = u_real.shape
    return stacked.reshape(lead_len, mode_len, row_len, 2, chan_len * chan_len)


def gelu_parts(pre_act):
    normal_cdf = 0.5 * (1.0 + lax.erf(pre_act * 0.7071067811865476))
    density = jnp.exp(-0.5 * pre_act * pre_act) * 0.3989422804014327
    return pre_act * normal_cdf, normal_cdf + pre_act * density


def analyze(sample_grid, table_in):
    spectrum = jnp.einsum('cxyz,zkp->xkpyc', sample_grid, table_in, preferred_element_type=jnp.float32)
    spectrum = spectral_lead(spectrum.reshape(NX, MZ, 2, NY * CHANNELS), NX, MX)
    return spectral_rows(spectrum.reshape(MX, MZ, 2, NY, CHANNELS), NY, MY)


def synthesize(spectrum, table_in):
    widened = synthesis_rows(spectrum, NY, MY).reshape(MX, MZ, 2, NY * CHANNELS)
    widened = synthesis_lead(widened, NX, MX).reshape(NX, MZ, 2, NY, CHANNELS)
    return jnp.einsum('xkpyc,kpz->cxyz', widened, table_in, precision=PRECISE)


def reference(field, cotangent, spectral_weight):
    weight = spectral_weight.reshape(MX, MZ, MY, 2, CHANNELS, CHANNELS)
    unit_scale = jnp.ones((MZ,), jnp.float32)
    depth_scale = depth_scales()
    forward_plain = depth_forward(unit_scale)
    forward_scaled = depth_forward(depth_scale)
    back_scaled = depth_inverse(depth_scale)
    back_plain = depth_inverse(unit_scale)

    def one_sample(sample_pair):
        sample_grid, grad_out = sample_pair
        spec_u = analyze(sample_grid, forward_plain)
        pre_act = synthesize(mix_modes(spec_u, weight), back_scaled)
        act_value, act_slope = gelu_parts(pre_act)
        grad_pre = (grad_out.astype(jnp.float32) * act_slope).astype(jnp.bfloat16)
        spec_g = analyze(grad_pre, forward_scaled)
        grad_grid = synthesize(mix_adjoint(spec_g, weight), back_plain)
        return act_value.astype(jnp.bfloat16), grad_grid.astype(jnp.bfloat16), weight_terms(spec_u, spec_g)

    out_all, grad_all, term_all = lax.map(one_sample, (field, cotangent))
    return out_all, grad_all, jnp.sum(term_all, axis=0)
```

```python
import functools
import math

import jax
import jax.numpy as jnp
import ml_dtypes
import numpy as np
from jax import lax
from jax.experimental import pallas as pl
from jax.experimental.pallas import tpu as pltpu
from jax.sharding import PartitionSpec as P

CHANNELS = 32
NX = 128
NY = 128
NZ = 128
MX = 16
MY = 16
MZ = 32
SAMPLES = 4
PAIR = 2
VMEM_BYTES = 56 * 1024 * 1024

NT = (((1,), (1,)), ((), ()))
NN = (((1,), (0,)), ((), ()))


def f32_dot(left_op, right_op, dims=NN):
    return lax.dot_general(left_op, right_op, dims, preferred_element_type=jnp.float32)


def mode_list(length, count):
    half_ids = np.arange(count // 2)
    return np.concatenate([half_ids, length - count // 2 + half_ids])


def split_pair(table):
    high = table.astype(np.float32).astype(ml_dtypes.bfloat16)
    low = (table - high.astype(np.float64)).astype(np.float32).astype(ml_dtypes.bfloat16)
    return high, low


def depth_scales():
    return np.where(np.arange(MZ) == 0, 1.0, 2.0) / float(NX * NY * NZ)


def plane_angles(x_cells, y_cells, blocks):
    kx = mode_list(NX, MX)
    ky = mode_list(NY, MY)
    turns_x = (kx[:, None] * x_cells[None, :] % NX) / NX
    turns_y = (ky[:, None] * y_cells[None, :] % NY) / NY
    turns = turns_x[:, None, :, None] + turns_y[None, :, None, :]
    turns = turns.reshape(blocks, MX // blocks * MY, x_cells.size * y_cells.size)
    return 2.0 * math.pi * turns


def plane_table(x_len, y_len, blocks):
    angles = plane_angles(np.arange(x_len), np.arange(y_len), blocks)
    table = np.stack([np.cos(angles), -np.sin(angles)], axis=1)
    return split_pair(table.reshape(2 * MX * MY, x_len * y_len))


def shift_tables(x_len, y_len, x_parts, y_parts):
    angles = plane_angles(np.arange(x_parts) * x_len, np.arange(y_parts) * y_len, y_parts)
    angles = np.moveaxis(angles, 2, 0)
    cosine = np.stack([np.cos(angles), np.cos(angles)], axis=2)
    signed = np.stack([np.sin(angles), -np.sin(angles)], axis=2)
    shape = (x_parts * y_parts, 1, 2 * MX * MY)
    return cosine.reshape(shape).astype(np.float32), signed.reshape(shape).astype(np.float32)


def depth_angles():
    turns = (np.arange(MZ)[:, None] * np.arange(NZ)[None, :] % NZ) / NZ
    return 2.0 * math.pi * turns


def analysis_table(scale_vec):
    angles = depth_angles()
    table = np.concatenate([np.cos(angles), np.sin(angles)]) * np.tile(scale_vec, 2)[:, None]
    table = table.astype(np.float32).astype(ml_dtypes.bfloat16)
    return np.concatenate([table, table], axis=1)


def synthesis_table(scale_vec):
    angles = depth_angles()
    table = np.concatenate([np.cos(angles), np.sin(angles)]) * np.tile(scale_vec, 2)[:, None]
    high, low = split_pair(table.T)
    return np.concatenate([high, high, low], axis=1)


def spread_input():
    one = np.repeat(np.eye(CHANNELS), CHANNELS, axis=1)
    return np.concatenate([one, one]).astype(ml_dtypes.bfloat16)


def spread_output():
    one = np.tile(np.eye(CHANNELS), (1, CHANNELS))
    return np.concatenate([one, one]).astype(ml_dtypes.bfloat16)


def halves(value):
    high = value.astype(jnp.bfloat16)
    low = (value - high.astype(jnp.float32)).astype(jnp.bfloat16)
    return high, low


def swap_parts(value):
    width = value.shape[1]
    blocks = [
        pltpu.roll(value[:, at : at + 128], 64, 1) for at in range(0, width, 128)
    ]
    return jnp.concatenate(blocks, axis=1)


def part_signs(width):
    lane_ids = lax.broadcasted_iota(jnp.int32, (1, width), 1)
    return jnp.where(lane_ids % 128 < 64, 1.0, -1.0).astype(jnp.float32)


def analyze_pair(grids, high_ref, low_ref, depth_ref, cos_ref, sin_ref, out_ref, x_parts, y_parts):
    plane = f32_dot(high_ref[...], grids) + f32_dot(low_ref[...], grids)
    signs = part_signs(plane.shape[0])
    mode_len = MZ // x_parts
    for chan in range(PAIR):
        high, low = halves(plane[:, chan * NZ : (chan + 1) * NZ])
        both = f32_dot(depth_ref[...], jnp.concatenate([high, low], axis=1), NT)
        spectrum = both[:MZ] + signs * swap_parts(both[MZ:])
        spectrum = spectrum * cos_ref[...] + swap_parts(spectrum) * sin_ref[...]
        for gx in range(x_parts):
            for gy in range(y_parts):
                out_ref[gx * y_parts + gy, chan] = spectrum[
                    gx * mode_len : (gx + 1) * mode_len, gy * 128 : (gy + 1) * 128
                ].astype(jnp.bfloat16)


def depth_fields(spec_ref, depth_ref, cos_ref, sin_ref, x_parts, y_parts):
    fields = []
    for chan in range(PAIR):
        rows = [
            jnp.concatenate(
                [spec_ref[gx * y_parts + gy, chan].astype(jnp.float32) for gy in range(y_parts)],
                axis=1,
            )
            for gx in range(x_parts)
        ]
        spectrum = jnp.concatenate(rows, axis=0)
        spectrum = spectrum * cos_ref[...] - swap_parts(spectrum) * sin_ref[...]
        turned = -part_signs(spectrum.shape[1]) * swap_parts(spectrum)
        high, low = halves(jnp.concatenate([spectrum, turned], axis=0))
        fields.append(
            f32_dot(depth_ref[...], jnp.concatenate([high, low, high], axis=0)).astype(jnp.bfloat16)
        )
    return jnp.concatenate(fields, axis=0)


def gelu_parts(pre_act):
    size = jnp.abs(pre_act)
    bell = jnp.exp(pre_act * pre_act * -0.5)
    turn = pl.reciprocal(1.0 + (0.3275911 * 0.7071067811865476) * size, approx=False)
    poly = 0.5 * 1.061405429 * turn - 0.5 * 1.453152027
    poly = poly * turn + 0.5 * 1.421413741
    poly = poly * turn - 0.5 * 0.284496736
    poly = poly * turn + 0.5 * 0.254829592
    tail = poly * turn * bell
    value = jnp.maximum(pre_act, 0.0) - size * tail
    normal_cdf = jnp.where(pre_act > 0.0, 1.0 - tail, tail)
    return value, normal_cdf + pre_act * bell * 0.3989422804014327


def analyze_kernel(x_parts, y_parts, grid_ref, high_ref, low_ref, depth_ref, cos_ref, sin_ref, out_ref):
    cells = grid_ref.shape[1] * grid_ref.shape[2]
    grids = jnp.concatenate(
        [grid_ref[chan].reshape(cells, NZ) for chan in range(PAIR)], axis=1
    )
    analyze_pair(
        grids, high_ref, low_ref, depth_ref, cos_ref, sin_ref, out_ref, x_parts, y_parts
    )


def turn_kernel(
    x_parts,
    y_parts,
    spec_ref,
    cot_ref,
    back_high_ref,
    back_low_ref,
    back_depth_ref,
    high_ref,
    low_ref,
    depth_ref,
    cos_ref,
    sin_ref,
    value_ref,
    out_ref,
    grad_ref,
):
    fields = depth_fields(spec_ref, back_depth_ref, cos_ref, sin_ref, x_parts, y_parts)
    x_len, y_len = cot_ref.shape[1], cot_ref.shape[2]
    step = min(8, x_len)
    for x_at in range(0, x_len, step):
        rows = slice(x_at * y_len, (x_at + step) * y_len)
        pre_act = f32_dot(back_high_ref[rows], fields, NT) + f32_dot(back_low_ref[rows], fields, NT)
        for chan in range(PAIR):
            lanes = slice(chan * NZ, (chan + 1) * NZ)
            value, slope = gelu_parts(pre_act[:, lanes])
            value_ref[chan, x_at : x_at + step] = value.astype(jnp.bfloat16).reshape(step, y_len, NZ)
            cotangent = cot_ref[chan, x_at : x_at + step].reshape(step * y_len, NZ)
            grad_ref[rows, lanes] = (cotangent.astype(jnp.float32) * slope).astype(jnp.bfloat16)
    analyze_pair(
        grad_ref[...], high_ref, low_ref, depth_ref, cos_ref, sin_ref, out_ref, x_parts, y_parts
    )


def synthesize_kernel(
    x_parts, y_parts, spec_ref, high_ref, low_ref, depth_ref, cos_ref, sin_ref, out_ref
):
    fields = depth_fields(spec_ref, depth_ref, cos_ref, sin_ref, x_parts, y_parts)
    x_len, y_len = out_ref.shape[1], out_ref.shape[2]
    step = min(8, x_len)
    for x_at in range(0, x_len, step):
        rows = slice(x_at * y_len, (x_at + step) * y_len)
        grid = f32_dot(high_ref[rows], fields, NT) + f32_dot(low_ref[rows], fields, NT)
        for chan in range(PAIR):
            out_ref[chan, x_at : x_at + step] = (
                grid[:, chan * NZ : (chan + 1) * NZ].astype(jnp.bfloat16).reshape(step, y_len, NZ)
            )


def mode_rows(value, spread_ref):
    high = value.astype(jnp.bfloat16).astype(jnp.float32)
    both = jnp.concatenate([high, value - high], axis=0)
    return f32_dot(both.T.astype(jnp.bfloat16), spread_ref[...])


def mix_kernel(
    adjoint, mode_len, step_len, recv_ref, weight_ref, spread_ref, gather_ref, spec_ref, out_ref,
    taken_ref, mixed_ref
):
    step_at = pl.program_id(0)

    @pl.when(step_at == 0)
    def _():
        total = recv_ref[0].astype(jnp.float32)
        for source in range(1, recv_ref.shape[0]):
            total = total + recv_ref[source].astype(jnp.float32)
        spec_ref[...] = total
        taken_ref[...] = total.reshape(taken_ref.shape)

    half = 64
    for at in range(step_len):
        mode_at = step_at * step_len + at
        here = pl.ds(mode_at, CHANNELS, stride=mode_len) if mode_len > 1 else slice(None)
        spread = mode_rows(taken_ref[here, :], spread_ref)
        real_in, imag_in = spread[:half], spread[half:]
        w_real = weight_ref[:, at, :, 0, :].reshape(half, CHANNELS * CHANNELS)
        w_imag = weight_ref[:, at, :, 1, :].reshape(half, CHANNELS * CHANNELS)
        if adjoint:
            real_part = real_in * w_real + imag_in * w_imag
            imag_part = imag_in * w_real - real_in * w_imag
            terms = jnp.concatenate([real_part, imag_part], axis=0)
        else:
            real_part = real_in * w_real - imag_in * w_imag
            imag_part = imag_in * w_real + real_in * w_imag
            terms = jnp.concatenate([real_part, imag_part], axis=0)
            width = terms.shape[1]
            while width > 128:
                width //= 2
                terms = terms[:, :width] + terms[:, width:]
        high, low = halves(terms)
        mixed = f32_dot(jnp.concatenate([high, low], axis=1), gather_ref[...])
        mixed_ref[here, :] = mixed.T[:CHANNELS]

    @pl.when(step_at == pl.num_programs(0) - 1)
    def _():
        out_ref[...] = mixed_ref[...].reshape(out_ref.shape).astype(jnp.bfloat16)


def weight_kernel(
    mode_len, step_len, u_ref, g_ref, pick_ref, spread_u_ref, spread_g_ref, out_ref
):
    step_at = pl.program_id(0)
    kx_len, row_len = out_ref.shape[0], out_ref.shape[2]
    half = kx_len * row_len

    def spread_rows(ref, here, spread_ref):
        value = ref[here, :]
        picked = []
        for sample in range(SAMPLES):
            high, low = halves(value[sample * CHANNELS : (sample + 1) * CHANNELS])
            both = jnp.concatenate([high, low], axis=1)
            picked.append(f32_dot(pick_ref[...], both, NT))
        high, low = halves(jnp.concatenate(picked, axis=0))
        return f32_dot(jnp.concatenate([high, low], axis=1), spread_ref[...])

    for at in range(step_len):
        mode_at = step_at * step_len + at
        rows = SAMPLES * CHANNELS
        here = pl.ds(mode_at, rows, stride=mode_len) if mode_len > 1 else slice(None)
        spread_u = spread_rows(u_ref, here, spread_u_ref)
        spread_g = spread_rows(g_ref, here, spread_g_ref)
        real_part, imag_part = 0.0, 0.0
        for sample in range(SAMPLES):
            top = sample * 2 * half
            u_real, u_imag = spread_u[top : top + half], spread_u[top + half : top + 2 * half]
            g_real, g_imag = spread_g[top : top + half], spread_g[top + half : top + 2 * half]
            real_part = real_part + (u_real * g_real + u_imag * g_imag)
            imag_part = imag_part + (u_real * g_imag - u_imag * g_real)
        for kx in range(kx_len):
            out_ref[kx, at, :, 0, :] = real_part[kx * row_len : (kx + 1) * row_len]
            out_ref[kx, at, :, 1, :] = imag_part[kx * row_len : (kx + 1) * row_len]


def whole_spec(array):
    zeros = (0,) * array.ndim
    return pl.BlockSpec(array.shape, lambda *at: zeros)


def params():
    return pltpu.CompilerParams(vmem_limit_bytes=VMEM_BYTES)


def cost(flops, bytes_accessed):
    return pl.CostEstimate(
        flops=int(flops), bytes_accessed=int(bytes_accessed), transcendentals=0
    )


def shards(x_parts, y_parts, field, cotangent, spectral_weight):
    chan_len, x_len, y_len = field.shape[1:4]
    kx_len, mode_len, row_len = spectral_weight.shape[:3]
    parts = x_parts * y_parts
    dp_len = lax.axis_size("dp")
    share_len = row_len // dp_len
    step_len = min(4, mode_len)

    high, low = plane_table(x_len, y_len, y_parts)
    back_high, back_low = high.T.copy(), low.T.copy()
    forward_plain = analysis_table(np.ones(MZ))
    forward_scaled = analysis_table(depth_scales())
    back_scaled = synthesis_table(depth_scales())
    back_plain = synthesis_table(np.ones(MZ))
    cosines, sines = shift_tables(x_len, y_len, x_parts, y_parts)
    place = lax.axis_index("gx") * y_parts + lax.axis_index("gy")
    shift_cos = lax.dynamic_index_in_dim(jnp.asarray(cosines), place, 0, False)
    shift_sin = lax.dynamic_index_in_dim(jnp.asarray(sines), place, 0, False)
    high, low, back_high, back_low = map(jnp.asarray, (high, low, back_high, back_low))

    pair_grid = pl.BlockSpec((PAIR, x_len, y_len, NZ), lambda at: (at, 0, 0, 0))
    pair_spec = pl.BlockSpec((parts, PAIR, mode_len, 128), lambda at: (0, at, 0, 0))
    grid_shape = jax.ShapeDtypeStruct((chan_len, x_len, y_len, NZ), jnp.bfloat16)
    spec_shape = jax.ShapeDtypeStruct((parts, chan_len, mode_len, 128), jnp.bfloat16)
    grid_bytes = chan_len * x_len * y_len * NZ * 2
    plane_flops = 2 * 2 * MX * MY * x_len * y_len * NZ * chan_len * 2

    def call(body, name, operands, specs, out_shapes, out_specs, scratch, flops, moved):
        return pl.pallas_call(
            functools.partial(body, x_parts, y_parts),
            name=name,
            grid=(chan_len // PAIR,),
            in_specs=specs,
            out_specs=out_specs,
            out_shape=out_shapes,
            scratch_shapes=scratch,
            compiler_params=params(),
            cost_estimate=cost(flops, moved),
        )(*operands)

    def tables_of(*arrays):
        return [whole_spec(array) for array in arrays]

    def mix(name, received, spread, gather, adjoint):
        small = (chan_len * mode_len, 128)
        return pl.pallas_call(
            functools.partial(mix_kernel, adjoint, mode_len, step_len),
            name=name,
            grid=(mode_len // step_len,),
            in_specs=[
                whole_spec(received),
                pl.BlockSpec(
                    (kx_len, step_len, row_len, 2, chan_len * chan_len),
                    lambda at: (0, at, 0, 0, 0),
                ),
                whole_spec(spread),
                whole_spec(gather),
            ],
            out_specs=[
                pl.BlockSpec((chan_len, mode_len, 128), lambda at: (0, 0, 0)),
                pl.BlockSpec((chan_len, mode_len, 128), lambda at: (0, 0, 0)),
            ],
            out_shape=[
                jax.ShapeDtypeStruct((chan_len, mode_len, 128), jnp.float32),
                jax.ShapeDtypeStruct((chan_len, mode_len, 128), jnp.bfloat16),
            ],
            scratch_shapes=[pltpu.VMEM(small, jnp.float32), pltpu.VMEM(small, jnp.float32)],
            compiler_params=params(),
            cost_estimate=cost(mode_len * 2e8, spectral_weight.size * 4),
        )(received, spectral_weight, spread, gather)

    def exchange(partial_sums):
        return lax.all_to_all(partial_sums, ("gx", "gy"), 0, 0, tiled=True)

    def collect(spectrum):
        return lax.all_gather(spectrum, ("gx", "gy"), axis=0, tiled=False)

    spread_in, spread_out = jnp.asarray(spread_input()), jnp.asarray(spread_output())
    onto_out = np.zeros((128, 128))
    onto_out[np.arange(128), np.arange(128) % CHANNELS] = 1.0
    onto_out = jnp.asarray(np.concatenate([onto_out, onto_out]).astype(ml_dtypes.bfloat16))
    onto_in = np.zeros((chan_len * chan_len, 128))
    onto_in[np.arange(chan_len * chan_len), np.arange(chan_len * chan_len) // CHANNELS] = 1.0
    onto_in = jnp.asarray(np.concatenate([onto_in, onto_in]).astype(ml_dtypes.bfloat16))

    partial_u = call(
        analyze_kernel,
        "analyze_field",
        (field[0], high, low, jnp.asarray(forward_plain), shift_cos, shift_sin),
        [pair_grid] + tables_of(high, low, forward_plain, shift_cos, shift_sin),
        spec_shape,
        pair_spec,
        [],
        plane_flops,
        grid_bytes,
    )
    spec_u, spec_v = mix("mix_forward", exchange(partial_u), spread_in, onto_out, False)
    gathered_u = lax.all_gather(spec_u, "dp", axis=0, tiled=False)
    out_grid, partial_g = call(
        turn_kernel,
        "activate",
        (
            collect(spec_v),
            cotangent[0],
            back_high,
            back_low,
            jnp.asarray(back_scaled),
            high,
            low,
            jnp.asarray(forward_scaled),
            shift_cos,
            shift_sin,
        ),
        [pair_spec, pair_grid]
        + tables_of(
            back_high, back_low, back_scaled, high, low, forward_scaled, shift_cos, shift_sin
        ),
        [grid_shape, spec_shape],
        [pair_grid, pair_spec],
        [pltpu.VMEM((x_len * y_len, PAIR * NZ), jnp.bfloat16)],
        3 * plane_flops,
        2 * grid_bytes,
    )
    spec_g, spec_du = mix("mix_adjoint", exchange(partial_g), spread_out, onto_in, True)
    gathered_g = lax.all_gather(spec_g, "dp", axis=0, tiled=False)
    grad_grid = call(
        synthesize_kernel,
        "synthesize_grad",
        (collect(spec_du), back_high, back_low, jnp.asarray(back_plain), shift_cos, shift_sin),
        [pair_spec] + tables_of(back_high, back_low, back_plain, shift_cos, shift_sin),
        grid_shape,
        pair_grid,
        [],
        plane_flops,
        grid_bytes,
    )

    lane_ids = np.arange(128)
    picks = np.zeros((dp_len, 2 * kx_len * share_len, 128))
    for rank in range(dp_len):
        rows = np.arange(2 * kx_len * share_len)
        lanes = rows // share_len * row_len + rank * share_len + rows % share_len
        picks[rank] = lanes[:, None] == lane_ids[None, :]
    picks = jnp.asarray(np.concatenate([picks, picks], axis=2).astype(ml_dtypes.bfloat16))
    pick = lax.dynamic_index_in_dim(picks, lax.axis_index("dp"), 0, False)
    flat = (dp_len * chan_len * mode_len, 128)
    all_u, all_g = gathered_u.reshape(flat), gathered_g.reshape(flat)
    weight_grad = pl.pallas_call(
        functools.partial(weight_kernel, mode_len, step_len),
        name="weight_terms",
        grid=(mode_len // step_len,),
        in_specs=[whole_spec(part) for part in (all_u, all_g, pick, spread_in, spread_out)],
        out_specs=pl.BlockSpec(
            (kx_len, step_len, share_len, 2, chan_len * chan_len), lambda at: (0, at, 0, 0, 0)
        ),
        out_shape=jax.ShapeDtypeStruct(
            (kx_len, mode_len, share_len, 2, chan_len * chan_len), jnp.float32
        ),
        compiler_params=params(),
        cost_estimate=cost(mode_len * 2e8, mode_len * 2e6),
    )(all_u, all_g, pick, spread_in, spread_out)
    return (out_grid[None], grad_grid[None], weight_grad)


def solution(mesh):
    placed = (
        P("dp", None, "gx", "gy", None),
        P("dp", None, "gx", "gy", None),
        P("gy", "gx", None, None, None),
    )
    return jax.shard_map(
        functools.partial(shards, mesh.shape["gx"], mesh.shape["gy"]),
        mesh=mesh,
        in_specs=placed,
        out_specs=(
            P("dp", None, "gx", "gy", None),
            P("dp", None, "gx", "gy", None),
            P("gy", "gx", "dp", None, None),
        ),
        check_vma=False,
    )
```

```python
import functools
import math

import jax
import jax.numpy as jnp
import ml_dtypes
import numpy as np
from jax import lax
from jax.experimental import pallas as pl
from jax.experimental.pallas import tpu as pltpu
from jax.sharding import PartitionSpec as P

CHANNELS = 32
NX = 128
NY = 128
NZ = 128
MX = 16
MY = 16
MZ = 32
SAMPLES = 4
PAIR = 2
CHUNKS = 2
PLANE_GAIN = 1.66526
VMEM_BYTES = 56 * 1024 * 1024

NT = (((1,), (1,)), ((), ()))
NN = (((1,), (0,)), ((), ()))


def f32_dot(left_op, right_op, dims=NN):
    return lax.dot_general(left_op, right_op, dims, preferred_element_type=jnp.float32)


def mode_list(length, count):
    half_ids = np.arange(count // 2)
    return np.concatenate([half_ids, length - count // 2 + half_ids])


def split_pair(table):
    high = table.astype(np.float32).astype(ml_dtypes.bfloat16)
    low = (table - high.astype(np.float64)).astype(np.float32).astype(ml_dtypes.bfloat16)
    return high, low


def depth_scales():
    return np.where(np.arange(MZ) == 0, 1.0, 2.0) / float(NX * NY * NZ)


def plane_angles(x_cells, y_cells, blocks):
    kx = mode_list(NX, MX)
    ky = mode_list(NY, MY)
    turns_x = (kx[:, None] * x_cells[None, :] % NX) / NX
    turns_y = (ky[:, None] * y_cells[None, :] % NY) / NY
    turns = turns_x[:, None, :, None] + turns_y[None, :, None, :]
    turns = turns.reshape(blocks, MX // blocks * MY, x_cells.size * y_cells.size)
    return 2.0 * math.pi * turns


def plane_table(x_len, y_len, blocks):
    angles = plane_angles(np.arange(x_len), np.arange(y_len), blocks)
    table = np.stack([np.cos(angles), -np.sin(angles)], axis=1)
    table = PLANE_GAIN * table.reshape(2 * MX * MY, x_len * y_len)
    return table.astype(np.float32).astype(ml_dtypes.bfloat16)


def plane_fit():
    exact = np.cos(2.0 * math.pi * np.arange(NX) / NX)
    rounded = (PLANE_GAIN * exact).astype(np.float32).astype(ml_dtypes.bfloat16)
    return (rounded.astype(np.float64) * exact).sum() / (exact * exact).sum()


def shift_tables(x_len, y_len, x_parts, y_parts):
    angles = plane_angles(np.arange(x_parts) * x_len, np.arange(y_parts) * y_len, y_parts)
    angles = np.moveaxis(angles, 2, 0)
    cosine = np.stack([np.cos(angles), np.cos(angles)], axis=2)
    signed = np.stack([np.sin(angles), -np.sin(angles)], axis=2)
    shape = (x_parts * y_parts, 1, 2 * MX * MY)
    cosine, signed = cosine / plane_fit(), signed / plane_fit()
    return cosine.reshape(shape).astype(np.float32), signed.reshape(shape).astype(np.float32)


def depth_angles():
    turns = (np.arange(MZ)[:, None] * np.arange(NZ)[None, :] % NZ) / NZ
    return 2.0 * math.pi * turns


def analysis_table(scale_vec):
    angles = depth_angles()
    table = np.concatenate([np.cos(angles), np.sin(angles)]) * np.tile(scale_vec, 2)[:, None]
    table = table.astype(np.float32).astype(ml_dtypes.bfloat16)
    return np.concatenate([table, table], axis=1)


def synthesis_table(scale_vec):
    angles = depth_angles()
    table = np.concatenate([np.cos(angles), np.sin(angles)]) * np.tile(scale_vec, 2)[:, None]
    high, low = split_pair(table.T)
    return np.concatenate([high, high, low], axis=1)


def spread_input():
    one = np.repeat(np.eye(CHANNELS), CHANNELS, axis=1)
    return np.concatenate([one, one]).astype(ml_dtypes.bfloat16)


def spread_output():
    one = np.tile(np.eye(CHANNELS), (1, CHANNELS))
    return np.concatenate([one, one]).astype(ml_dtypes.bfloat16)


def halves(value):
    high = value.astype(jnp.bfloat16)
    low = (value - high.astype(jnp.float32)).astype(jnp.bfloat16)
    return high, low


def swap_parts(value):
    width = value.shape[1]
    blocks = [
        pltpu.roll(value[:, at : at + 128], 64, 1) for at in range(0, width, 128)
    ]
    return jnp.concatenate(blocks, axis=1)


def part_signs(width):
    lane_ids = lax.broadcasted_iota(jnp.int32, (1, width), 1)
    return jnp.where(lane_ids % 128 < 64, 1.0, -1.0).astype(jnp.float32)


def analyze_pair(grids, plane_ref, depth_ref, cos_ref, sin_ref, out_ref, x_parts, y_parts):
    plane = f32_dot(plane_ref[...], grids)
    signs = part_signs(plane.shape[0])
    mode_len = MZ // x_parts
    for chan in range(PAIR):
        high, low = halves(plane[:, chan * NZ : (chan + 1) * NZ])
        both = f32_dot(depth_ref[...], jnp.concatenate([high, low], axis=1), NT)
        spectrum = both[:MZ] + signs * swap_parts(both[MZ:])
        spectrum = spectrum * cos_ref[...] + swap_parts(spectrum) * sin_ref[...]
        for gx in range(x_parts):
            for gy in range(y_parts):
                out_ref[gx * y_parts + gy, chan] = spectrum[
                    gx * mode_len : (gx + 1) * mode_len, gy * 128 : (gy + 1) * 128
                ].astype(jnp.bfloat16)


def depth_fields(spec_ref, depth_ref, cos_ref, sin_ref, x_parts, y_parts):
    fields = []
    for chan in range(PAIR):
        rows = [
            jnp.concatenate(
                [spec_ref[gx * y_parts + gy, chan].astype(jnp.float32) for gy in range(y_parts)],
                axis=1,
            )
            for gx in range(x_parts)
        ]
        spectrum = jnp.concatenate(rows, axis=0)
        spectrum = spectrum * cos_ref[...] - swap_parts(spectrum) * sin_ref[...]
        turned = -part_signs(spectrum.shape[1]) * swap_parts(spectrum)
        high, low = halves(jnp.concatenate([spectrum, turned], axis=0))
        fields.append(
            f32_dot(depth_ref[...], jnp.concatenate([high, low, high], axis=0)).astype(jnp.bfloat16)
        )
    return jnp.concatenate(fields, axis=0)


def gelu_parts(pre_act):
    size = jnp.abs(pre_act)
    bell = jnp.exp(pre_act * pre_act * -0.5)
    turn = pl.reciprocal(1.0 + (0.3275911 * 0.7071067811865476) * size, approx=False)
    poly = 0.5 * 1.061405429 * turn - 0.5 * 1.453152027
    poly = poly * turn + 0.5 * 1.421413741
    poly = poly * turn - 0.5 * 0.284496736
    poly = poly * turn + 0.5 * 0.254829592
    tail = poly * turn * bell
    value = jnp.maximum(pre_act, 0.0) - size * tail
    normal_cdf = jnp.where(pre_act > 0.0, 1.0 - tail, tail)
    return value, normal_cdf + pre_act * bell * 0.3989422804014327


def analyze_kernel(x_parts, y_parts, grid_ref, plane_ref, depth_ref, cos_ref, sin_ref, out_ref):
    cells = grid_ref.shape[1] * grid_ref.shape[2]
    grids = jnp.concatenate(
        [grid_ref[chan].reshape(cells, NZ) for chan in range(PAIR)], axis=1
    )
    analyze_pair(grids, plane_ref, depth_ref, cos_ref, sin_ref, out_ref, x_parts, y_parts)


def activate_kernel(
    x_parts,
    y_parts,
    spec_ref,
    cot_ref,
    back_ref,
    back_depth_ref,
    plane_ref,
    depth_ref,
    cos_ref,
    sin_ref,
    *rest,
):
    value_ref, out_ref, grad_ref = rest[-3:]
    fields = depth_fields(spec_ref, back_depth_ref, cos_ref, sin_ref, x_parts, y_parts)
    x_len, y_len = cot_ref.shape[1], cot_ref.shape[2]
    step = min(8, x_len)
    for x_at in range(0, x_len, step):
        rows = slice(x_at * y_len, (x_at + step) * y_len)
        pre_act = f32_dot(back_ref[rows], fields, NT)
        for chan in range(PAIR):
            lanes = slice(chan * NZ, (chan + 1) * NZ)
            value, slope = gelu_parts(pre_act[:, lanes])
            value_ref[chan, x_at : x_at + step] = value.astype(jnp.bfloat16).reshape(step, y_len, NZ)
            cotangent = cot_ref[chan, x_at : x_at + step].reshape(step * y_len, NZ)
            grad_ref[rows, lanes] = (cotangent.astype(jnp.float32) * slope).astype(jnp.bfloat16)
    analyze_pair(
        grad_ref[...], plane_ref, depth_ref, cos_ref, sin_ref, out_ref, x_parts, y_parts
    )


def synthesize_kernel(
    x_parts, y_parts, spec_ref, back_ref, depth_ref, cos_ref, sin_ref, *rest
):
    out_ref = rest[-1]
    fields = depth_fields(spec_ref, depth_ref, cos_ref, sin_ref, x_parts, y_parts)
    x_len, y_len = out_ref.shape[1], out_ref.shape[2]
    step = min(8, x_len)
    for x_at in range(0, x_len, step):
        rows = slice(x_at * y_len, (x_at + step) * y_len)
        grid = f32_dot(back_ref[rows], fields, NT)
        for chan in range(PAIR):
            out_ref[chan, x_at : x_at + step] = (
                grid[:, chan * NZ : (chan + 1) * NZ].astype(jnp.bfloat16).reshape(step, y_len, NZ)
            )


def mode_rows(value, spread_ref):
    high = value.astype(jnp.bfloat16).astype(jnp.float32)
    both = jnp.concatenate([high, value - high], axis=0)
    return f32_dot(both.T.astype(jnp.bfloat16), spread_ref[...])


def mix_kernel(adjoint, mode_len, step_len, *refs):
    recv_refs, refs = refs[:CHUNKS], refs[CHUNKS:]
    weight_ref, spread_ref, gather_ref, share_ref, *refs = refs
    kept_ref, refs = (refs[0], refs[1:]) if adjoint else (None, refs)
    send_ref, out_refs = refs[0], refs[1 : 1 + CHUNKS]
    taken_ref, mixed_ref = refs[1 + CHUNKS :]
    chunk_len = CHANNELS // CHUNKS
    step_at = pl.program_id(0)

    @pl.when(step_at == 0)
    def _():
        for chunk, recv_ref in enumerate(recv_refs):
            total = recv_ref[0].astype(jnp.float32)
            for source in range(1, recv_ref.shape[0]):
                total = total + recv_ref[source].astype(jnp.float32)
            rows = chunk_len * mode_len
            taken_ref[chunk * rows : (chunk + 1) * rows] = total.reshape(rows, 128)

    half = 64
    inputs = []
    for at in range(step_len):
        mode_at = step_at * step_len + at
        here = pl.ds(mode_at, CHANNELS, stride=mode_len) if mode_len > 1 else slice(None)
        taken = taken_ref[here, :]
        inputs.append(taken)
        spread = mode_rows(taken, spread_ref)
        real_in, imag_in = spread[:half], spread[half:]
        w_real = weight_ref[:, at, :, 0, :].reshape(half, CHANNELS * CHANNELS)
        w_imag = weight_ref[:, at, :, 1, :].reshape(half, CHANNELS * CHANNELS)
        if adjoint:
            real_part = real_in * w_real + imag_in * w_imag
            imag_part = imag_in * w_real - real_in * w_imag
            terms = jnp.concatenate([real_part, imag_part], axis=0)
        else:
            real_part = real_in * w_real - imag_in * w_imag
            imag_part = imag_in * w_real + real_in * w_imag
            terms = jnp.concatenate([real_part, imag_part], axis=0)
            width = terms.shape[1]
            while width > 128:
                width //= 2
                terms = terms[:, :width] + terms[:, width:]
        high, low = halves(terms)
        mixed = f32_dot(jnp.concatenate([high, low], axis=1), gather_ref[...])
        mixed_ref[here, :] = mixed.T[:CHANNELS]

    high, low = halves(jnp.concatenate(inputs, axis=1))
    shared = f32_dot(jnp.concatenate([high, low], axis=0), share_ref[...])
    shared = shared[:CHANNELS] + shared[CHANNELS:]
    lanes = send_ref.shape[-1]
    for rank in range(send_ref.shape[0]):
        part = shared[:, rank * lanes : (rank + 1) * lanes]
        if adjoint:
            send_ref[rank, 0, 0] = kept_ref[rank, 0]
            send_ref[rank, 0, 1] = part
        else:
            send_ref[rank, 0] = part

    @pl.when(step_at == pl.num_programs(0) - 1)
    def _():
        rows = chunk_len * mode_len
        for chunk, out_ref in enumerate(out_refs):
            part = mixed_ref[chunk * rows : (chunk + 1) * rows]
            out_ref[...] = part.reshape(out_ref.shape).astype(jnp.bfloat16)


def weight_kernel(terms_ref, spread_u_ref, spread_g_ref, out_ref):
    kx_len, step_len, row_len = out_ref.shape[:3]
    half = kx_len * row_len
    real_part, imag_part = 0.0, 0.0
    for sample in range(terms_ref.shape[0]):
        shape = (step_len, 2, half, CHANNELS * CHANNELS)
        spread_u = mode_rows(terms_ref[sample, 0, 0], spread_u_ref).reshape(shape)
        spread_g = mode_rows(terms_ref[sample, 0, 1], spread_g_ref).reshape(shape)
        u_real, u_imag = spread_u[:, 0], spread_u[:, 1]
        g_real, g_imag = spread_g[:, 0], spread_g[:, 1]
        real_part = real_part + (u_real * g_real + u_imag * g_imag)
        imag_part = imag_part + (u_real * g_imag - u_imag * g_real)
    for at in range(step_len):
        for kx in range(kx_len):
            rows = slice(kx * row_len, (kx + 1) * row_len)
            out_ref[kx, at, :, 0, :] = real_part[at, rows]
            out_ref[kx, at, :, 1, :] = imag_part[at, rows]


def whole_spec(array):
    zeros = (0,) * array.ndim
    return pl.BlockSpec(array.shape, lambda *at: zeros)


def params():
    return pltpu.CompilerParams(vmem_limit_bytes=VMEM_BYTES)


def cost(flops, bytes_accessed):
    return pl.CostEstimate(
        flops=int(flops), bytes_accessed=int(bytes_accessed), transcendentals=0
    )


def share_table(step_len, kx_len, row_len, share_len):
    ids = np.arange(step_len * 2 * kx_len * row_len)
    ids = ids.reshape(step_len * 2 * kx_len, row_len // share_len, share_len)
    ids = np.moveaxis(ids, 1, 0).reshape(-1)
    return (np.arange(ids.size)[:, None] == ids[None, :]).astype(ml_dtypes.bfloat16)


def shards(x_parts, y_parts, field, cotangent, spectral_weight):
    chan_len, x_len, y_len = field.shape[1:4]
    kx_len, mode_len, row_len = spectral_weight.shape[:3]
    parts = x_parts * y_parts
    dp_len = lax.axis_size("dp")
    share_len = row_len // dp_len
    step_len = min(4, mode_len)
    chunk_len = chan_len // CHUNKS
    chunk_steps = chunk_len // PAIR

    plane = plane_table(x_len, y_len, y_parts)
    back = jnp.asarray(plane.T.copy())
    plane = jnp.asarray(plane)
    forward_plain = jnp.asarray(analysis_table(np.ones(MZ)))
    forward_scaled = jnp.asarray(analysis_table(depth_scales()))
    back_scaled = jnp.asarray(synthesis_table(depth_scales()))
    back_plain = jnp.asarray(synthesis_table(np.ones(MZ)))
    cosines, sines = shift_tables(x_len, y_len, x_parts, y_parts)
    place = lax.axis_index("gx") * y_parts + lax.axis_index("gy")
    shift_cos = lax.dynamic_index_in_dim(jnp.asarray(cosines), place, 0, False)
    shift_sin = lax.dynamic_index_in_dim(jnp.asarray(sines), place, 0, False)

    pair_spec = pl.BlockSpec((parts, PAIR, mode_len, 128), lambda at: (0, at, 0, 0))
    grid_shape = jax.ShapeDtypeStruct((chan_len, x_len, y_len, NZ), jnp.bfloat16)
    spec_shape = jax.ShapeDtypeStruct((parts, chunk_len, mode_len, 128), jnp.bfloat16)
    grid_bytes = chunk_len * x_len * y_len * NZ * 2
    plane_flops = 2 * 2 * MX * MY * x_len * y_len * NZ * chunk_len * 2

    def pair_grid(chunk):
        return pl.BlockSpec(
            (PAIR, x_len, y_len, NZ), lambda at: (at + chunk * chunk_steps, 0, 0, 0)
        )

    def tables_of(*arrays):
        return [whole_spec(array) for array in arrays]

    def call(body, name, operands, specs, earlier, out_shapes, out_specs, scratch, flops, moved):
        aliases = {}
        if earlier is not None:
            aliases = {len(operands): 0}
            operands = (*operands, earlier)
            specs = [*specs, pl.BlockSpec(memory_space=pl.ANY)]
        return pl.pallas_call(
            functools.partial(body, x_parts, y_parts),
            name=name,
            grid=(chunk_steps,),
            in_specs=specs,
            out_specs=out_specs,
            out_shape=out_shapes,
            scratch_shapes=scratch,
            input_output_aliases=aliases,
            compiler_params=params(),
            cost_estimate=cost(flops, moved),
        )(*operands)

    def mix(name, received, spread, gather, kept):
        adjoint = kept is not None
        steps = mode_len // step_len
        lanes = step_len * 2 * kx_len * share_len
        small = (chan_len * mode_len, 128)
        operands = [*received, spectral_weight, spread, gather, share]
        specs = [
            *tables_of(*received),
            pl.BlockSpec(
                (kx_len, step_len, row_len, 2, chan_len * chan_len), lambda at: (0, at, 0, 0, 0)
            ),
            *tables_of(spread, gather, share),
        ]
        one_send = pl.BlockSpec((dp_len, 1, chan_len, lanes), lambda at: (0, at, 0, 0))
        if adjoint:
            operands.append(kept)
            specs.append(one_send)
            send_shape = (dp_len, steps, 2, chan_len, lanes)
            send_spec = pl.BlockSpec((dp_len, 1, 2, chan_len, lanes), lambda at: (0, at, 0, 0, 0))
        else:
            send_shape = (dp_len, steps, chan_len, lanes)
            send_spec = one_send
        chunk_shape = (chunk_len, mode_len, 128)
        return pl.pallas_call(
            functools.partial(mix_kernel, adjoint, mode_len, step_len),
            name=name,
            grid=(steps,),
            in_specs=specs,
            out_specs=[send_spec]
            + [pl.BlockSpec(chunk_shape, lambda at: (0, 0, 0)) for _ in range(CHUNKS)],
            out_shape=[jax.ShapeDtypeStruct(send_shape, jnp.float32)]
            + [jax.ShapeDtypeStruct(chunk_shape, jnp.bfloat16) for _ in range(CHUNKS)],
            scratch_shapes=[pltpu.VMEM(small, jnp.float32), pltpu.VMEM(small, jnp.float32)],
            compiler_params=params(),
            cost_estimate=cost(mode_len * 2e8, spectral_weight.size * 4),
        )(*operands)

    def exchange(partial_sums):
        return lax.all_to_all(partial_sums, ("gx", "gy"), 0, 0, tiled=True)

    def collect(spectrum):
        return lax.all_gather(spectrum, ("gx", "gy"), axis=0, tiled=False)

    share = jnp.asarray(share_table(step_len, kx_len, row_len, share_len))
    spread_in, spread_out = jnp.asarray(spread_input()), jnp.asarray(spread_output())
    onto_out = np.zeros((128, 128))
    onto_out[np.arange(128), np.arange(128) % CHANNELS] = 1.0
    onto_out = jnp.asarray(np.concatenate([onto_out, onto_out]).astype(ml_dtypes.bfloat16))
    onto_in = np.zeros((chan_len * chan_len, 128))
    onto_in[np.arange(chan_len * chan_len), np.arange(chan_len * chan_len) // CHANNELS] = 1.0
    onto_in = jnp.asarray(np.concatenate([onto_in, onto_in]).astype(ml_dtypes.bfloat16))

    received = []
    tables = (plane, forward_plain, shift_cos, shift_sin)
    for chunk in range(CHUNKS):
        partial_u = call(
            analyze_kernel,
            "analyze_field",
            (field[0], *tables),
            [pair_grid(chunk), *tables_of(*tables)],
            None,
            spec_shape,
            pair_spec,
            [],
            plane_flops,
            grid_bytes,
        )
        received.append(exchange(partial_u))
    send_u, *spec_v = mix("mix_forward", received, spread_in, onto_out, None)

    received, out_grid = [], None
    gathered = [collect(spectrum) for spectrum in spec_v]
    tables = (back, back_scaled, plane, forward_scaled, shift_cos, shift_sin)
    for chunk in range(CHUNKS):
        out_grid, partial_g = call(
            activate_kernel,
            "activate",
            (gathered[chunk], cotangent[0], *tables),
            [pair_spec, pair_grid(chunk), *tables_of(*tables)],
            out_grid,
            [grid_shape, spec_shape],
            [pair_grid(chunk), pair_spec],
            [pltpu.VMEM((x_len * y_len, PAIR * NZ), jnp.bfloat16)],
            4 * plane_flops,
            2 * grid_bytes,
        )
        received.append(exchange(partial_g))
    send_terms, *spec_du = mix("mix_adjoint", received, spread_out, onto_in, send_u)

    gathered = [collect(spectrum) for spectrum in spec_du]
    terms = lax.all_to_all(send_terms, "dp", 0, 0, tiled=True)
    lanes = terms.shape[-1]
    weight_grad = pl.pallas_call(
        weight_kernel,
        name="weight_terms",
        grid=(mode_len // step_len,),
        in_specs=[
            pl.BlockSpec((dp_len, 1, 2, chan_len, lanes), lambda at: (0, at, 0, 0, 0)),
            *tables_of(spread_in, spread_out),
        ],
        out_specs=pl.BlockSpec(
            (kx_len, step_len, share_len, 2, chan_len * chan_len), lambda at: (0, at, 0, 0, 0)
        ),
        out_shape=jax.ShapeDtypeStruct(
            (kx_len, mode_len, share_len, 2, chan_len * chan_len), jnp.float32
        ),
        compiler_params=params(),
        cost_estimate=cost(mode_len * 2e8, mode_len * 2e6),
    )(terms, spread_in, spread_out)

    grad_grid = None
    tables = (back, back_plain, shift_cos, shift_sin)
    for chunk in range(CHUNKS):
        grad_grid = call(
            synthesize_kernel,
            "synthesize_grad",
            (gathered[chunk], *tables),
            [pair_spec, *tables_of(*tables)],
            grad_grid,
            grid_shape,
            pair_grid(chunk),
            [],
            plane_flops,
            grid_bytes,
        )
    return (out_grid[None], grad_grid[None], weight_grad)


def solution(mesh):
    placed = (
        P("dp", None, "gx", "gy", None),
        P("dp", None, "gx", "gy", None),
        P("gy", "gx", None, None, None),
    )
    return jax.shard_map(
        functools.partial(shards, mesh.shape["gx"], mesh.shape["gy"]),
        mesh=mesh,
        in_specs=placed,
        out_specs=(
            P("dp", None, "gx", "gy", None),
            P("dp", None, "gx", "gy", None),
            P("gy", "gx", "dp", None, None),
        ),
        check_vma=False,
    )
```

```python
import functools
import math

import jax
import jax.numpy as jnp
import ml_dtypes
import numpy as np
from jax import lax
from jax.experimental import pallas as pl
from jax.experimental.pallas import tpu as pltpu
from jax.sharding import PartitionSpec as P

CHANNELS = 32
NX = 128
NY = 128
NZ = 128
MX = 16
MY = 16
MZ = 32
SAMPLES = 4
PAIR = 2
ANALYZE_CHUNKS = (8, 12, 12)
ACTIVATE_CHUNKS = (8, 16, 8)
SYNTHESIZE_CHUNKS = (8, 16, 8)
PLANE_GAIN = 1.66526
VMEM_BYTES = 56 * 1024 * 1024

NT = (((1,), (1,)), ((), ()))
NN = (((1,), (0,)), ((), ()))


def f32_dot(left_op, right_op, dims=NN):
    return lax.dot_general(left_op, right_op, dims, preferred_element_type=jnp.float32)


def mode_list(length, count):
    half_ids = np.arange(count // 2)
    return np.concatenate([half_ids, length - count // 2 + half_ids])


def split_pair(table):
    high = table.astype(np.float32).astype(ml_dtypes.bfloat16)
    low = (table - high.astype(np.float64)).astype(np.float32).astype(ml_dtypes.bfloat16)
    return high, low


def depth_scales():
    return np.where(np.arange(MZ) == 0, 1.0, 2.0) / float(NX * NY * NZ)


def plane_angles(x_cells, y_cells, blocks):
    kx = mode_list(NX, MX)
    ky = mode_list(NY, MY)
    turns_x = (kx[:, None] * x_cells[None, :] % NX) / NX
    turns_y = (ky[:, None] * y_cells[None, :] % NY) / NY
    turns = turns_x[:, None, :, None] + turns_y[None, :, None, :]
    turns = turns.reshape(blocks, MX // blocks * MY, x_cells.size * y_cells.size)
    return 2.0 * math.pi * turns


def plane_table(x_len, y_len, blocks):
    angles = plane_angles(np.arange(x_len), np.arange(y_len), blocks)
    table = np.stack([np.cos(angles), -np.sin(angles)], axis=1)
    table = PLANE_GAIN * table.reshape(2 * MX * MY, x_len * y_len)
    return table.astype(np.float32).astype(ml_dtypes.bfloat16)


def plane_fit():
    exact = np.cos(2.0 * math.pi * np.arange(NX) / NX)
    rounded = (PLANE_GAIN * exact).astype(np.float32).astype(ml_dtypes.bfloat16)
    return (rounded.astype(np.float64) * exact).sum() / (exact * exact).sum()


def shift_tables(x_len, y_len, x_parts, y_parts):
    angles = plane_angles(np.arange(x_parts) * x_len, np.arange(y_parts) * y_len, y_parts)
    angles = np.moveaxis(angles, 2, 0)
    cosine = np.stack([np.cos(angles), np.cos(angles)], axis=2)
    signed = np.stack([np.sin(angles), -np.sin(angles)], axis=2)
    shape = (x_parts * y_parts, 1, 2 * MX * MY)
    cosine, signed = cosine / plane_fit(), signed / plane_fit()
    return cosine.reshape(shape).astype(np.float32), signed.reshape(shape).astype(np.float32)


def depth_angles():
    turns = (np.arange(MZ)[:, None] * np.arange(NZ)[None, :] % NZ) / NZ
    return 2.0 * math.pi * turns


def analysis_table(scale_vec):
    angles = depth_angles()
    table = np.concatenate([np.cos(angles), np.sin(angles)]) * np.tile(scale_vec, 2)[:, None]
    table = table.astype(np.float32).astype(ml_dtypes.bfloat16)
    return np.concatenate([table, table], axis=1)


def synthesis_table(scale_vec):
    angles = depth_angles()
    table = np.concatenate([np.cos(angles), np.sin(angles)]) * np.tile(scale_vec, 2)[:, None]
    high, low = split_pair(table.T)
    return np.concatenate([high, high, low], axis=1)


def spread_input():
    one = np.repeat(np.eye(CHANNELS), CHANNELS, axis=1)
    return np.concatenate([one, one]).astype(ml_dtypes.bfloat16)


def spread_output():
    one = np.tile(np.eye(CHANNELS), (1, CHANNELS))
    return np.concatenate([one, one]).astype(ml_dtypes.bfloat16)


def halves(value):
    high = value.astype(jnp.bfloat16)
    low = (value - high.astype(jnp.float32)).astype(jnp.bfloat16)
    return high, low


def swap_parts(value):
    width = value.shape[1]
    blocks = [
        pltpu.roll(value[:, at : at + 128], 64, 1) for at in range(0, width, 128)
    ]
    return jnp.concatenate(blocks, axis=1)


def part_signs(width):
    lane_ids = lax.broadcasted_iota(jnp.int32, (1, width), 1)
    return jnp.where(lane_ids % 128 < 64, 1.0, -1.0).astype(jnp.float32)


def analyze_pair(grids, plane_ref, depth_ref, cos_ref, sin_ref, out_ref, x_parts, y_parts):
    plane = f32_dot(plane_ref[...], grids)
    signs = part_signs(plane.shape[0])
    mode_len = MZ // x_parts
    for chan in range(PAIR):
        high, low = halves(plane[:, chan * NZ : (chan + 1) * NZ])
        both = f32_dot(depth_ref[...], jnp.concatenate([high, low], axis=1), NT)
        spectrum = both[:MZ] + signs * swap_parts(both[MZ:])
        spectrum = spectrum * cos_ref[...] + swap_parts(spectrum) * sin_ref[...]
        for gx in range(x_parts):
            for gy in range(y_parts):
                out_ref[gx * y_parts + gy, chan] = spectrum[
                    gx * mode_len : (gx + 1) * mode_len, gy * 128 : (gy + 1) * 128
                ].astype(jnp.bfloat16)


def depth_fields(spec_ref, depth_ref, cos_ref, sin_ref, x_parts, y_parts):
    fields = []
    for chan in range(PAIR):
        rows = [
            jnp.concatenate(
                [spec_ref[gx * y_parts + gy, chan].astype(jnp.float32) for gy in range(y_parts)],
                axis=1,
            )
            for gx in range(x_parts)
        ]
        spectrum = jnp.concatenate(rows, axis=0)
        spectrum = spectrum * cos_ref[...] - swap_parts(spectrum) * sin_ref[...]
        turned = -part_signs(spectrum.shape[1]) * swap_parts(spectrum)
        high, low = halves(jnp.concatenate([spectrum, turned], axis=0))
        fields.append(
            f32_dot(depth_ref[...], jnp.concatenate([high, low, high], axis=0)).astype(jnp.bfloat16)
        )
    return jnp.concatenate(fields, axis=0)


def gelu_parts(pre_act):
    size = jnp.abs(pre_act)
    bell = jnp.exp(pre_act * pre_act * -0.5)
    turn = pl.reciprocal(1.0 + (0.3275911 * 0.7071067811865476) * size, approx=False)
    poly = 0.5 * 1.061405429 * turn - 0.5 * 1.453152027
    poly = poly * turn + 0.5 * 1.421413741
    poly = poly * turn - 0.5 * 0.284496736
    poly = poly * turn + 0.5 * 0.254829592
    tail = poly * turn * bell
    value = jnp.maximum(pre_act, 0.0) - size * tail
    normal_cdf = jnp.where(pre_act > 0.0, 1.0 - tail, tail)
    return value, normal_cdf + pre_act * bell * 0.3989422804014327


def analyze_kernel(x_parts, y_parts, grid_ref, plane_ref, depth_ref, cos_ref, sin_ref, out_ref):
    cells = grid_ref.shape[1] * grid_ref.shape[2]
    grids = jnp.concatenate(
        [grid_ref[chan].reshape(cells, NZ) for chan in range(PAIR)], axis=1
    )
    analyze_pair(grids, plane_ref, depth_ref, cos_ref, sin_ref, out_ref, x_parts, y_parts)


def activate_kernel(
    x_parts,
    y_parts,
    spec_ref,
    cot_ref,
    back_ref,
    back_depth_ref,
    plane_ref,
    depth_ref,
    cos_ref,
    sin_ref,
    *rest,
):
    value_ref, out_ref, grad_ref = rest[-3:]
    fields = depth_fields(spec_ref, back_depth_ref, cos_ref, sin_ref, x_parts, y_parts)
    x_len, y_len = cot_ref.shape[1], cot_ref.shape[2]
    step = min(8, x_len)
    for x_at in range(0, x_len, step):
        rows = slice(x_at * y_len, (x_at + step) * y_len)
        pre_act = f32_dot(back_ref[rows], fields, NT)
        for chan in range(PAIR):
            lanes = slice(chan * NZ, (chan + 1) * NZ)
            value, slope = gelu_parts(pre_act[:, lanes])
            value_ref[chan, x_at : x_at + step] = value.astype(jnp.bfloat16).reshape(step, y_len, NZ)
            cotangent = cot_ref[chan, x_at : x_at + step].reshape(step * y_len, NZ)
            grad_ref[rows, lanes] = (cotangent.astype(jnp.float32) * slope).astype(jnp.bfloat16)
    analyze_pair(
        grad_ref[...], plane_ref, depth_ref, cos_ref, sin_ref, out_ref, x_parts, y_parts
    )


def synthesize_kernel(
    x_parts, y_parts, spec_ref, back_ref, depth_ref, cos_ref, sin_ref, *rest
):
    out_ref = rest[-1]
    fields = depth_fields(spec_ref, depth_ref, cos_ref, sin_ref, x_parts, y_parts)
    x_len, y_len = out_ref.shape[1], out_ref.shape[2]
    step = min(8, x_len)
    for x_at in range(0, x_len, step):
        rows = slice(x_at * y_len, (x_at + step) * y_len)
        grid = f32_dot(back_ref[rows], fields, NT)
        for chan in range(PAIR):
            out_ref[chan, x_at : x_at + step] = (
                grid[:, chan * NZ : (chan + 1) * NZ].astype(jnp.bfloat16).reshape(step, y_len, NZ)
            )


def mode_rows(value, spread_ref):
    high = value.astype(jnp.bfloat16).astype(jnp.float32)
    both = jnp.concatenate([high, value - high], axis=0)
    return f32_dot(both.T.astype(jnp.bfloat16), spread_ref[...])


def spans(chunks):
    ends = np.cumsum(chunks)
    return [(int(end) - size, int(end)) for size, end in zip(chunks, ends)]


def mix_kernel(adjoint, mode_len, step_len, taken, given, *refs):
    recv_refs, refs = refs[: len(taken)], refs[len(taken) :]
    weight_ref, spread_ref, gather_ref, share_ref, *refs = refs
    kept_ref, refs = (refs[0], refs[1:]) if adjoint else (None, refs)
    send_ref, *out_refs, taken_ref, mixed_ref = refs
    step_at = pl.program_id(0)

    @pl.when(step_at == 0)
    def _():
        for (start, stop), recv_ref in zip(spans(taken), recv_refs):
            total = recv_ref[0].astype(jnp.float32)
            for source in range(1, recv_ref.shape[0]):
                total = total + recv_ref[source].astype(jnp.float32)
            rows = slice(start * mode_len, stop * mode_len)
            taken_ref[rows] = total.reshape((stop - start) * mode_len, 128)

    half = 64
    inputs = []
    for at in range(step_len):
        mode_at = step_at * step_len + at
        here = pl.ds(mode_at, CHANNELS, stride=mode_len) if mode_len > 1 else slice(None)
        inputs.append(taken_ref[here, :])
        spread = mode_rows(inputs[-1], spread_ref)
        real_in, imag_in = spread[:half], spread[half:]
        w_real = weight_ref[:, at, :, 0, :].reshape(half, CHANNELS * CHANNELS)
        w_imag = weight_ref[:, at, :, 1, :].reshape(half, CHANNELS * CHANNELS)
        if adjoint:
            real_part = real_in * w_real + imag_in * w_imag
            imag_part = imag_in * w_real - real_in * w_imag
            terms = jnp.concatenate([real_part, imag_part], axis=0)
        else:
            real_part = real_in * w_real - imag_in * w_imag
            imag_part = imag_in * w_real + real_in * w_imag
            terms = jnp.concatenate([real_part, imag_part], axis=0)
            width = terms.shape[1]
            while width > 128:
                width //= 2
                terms = terms[:, :width] + terms[:, width:]
        high, low = halves(terms)
        mixed = f32_dot(jnp.concatenate([high, low], axis=1), gather_ref[...])
        mixed_ref[here, :] = mixed.T[:CHANNELS]

    high, low = halves(jnp.concatenate(inputs, axis=1))
    shared = f32_dot(jnp.concatenate([high, low], axis=0), share_ref[...])
    shared = shared[:CHANNELS] + shared[CHANNELS:]
    lanes = send_ref.shape[-1]
    for rank in range(send_ref.shape[0]):
        part = shared[:, rank * lanes : (rank + 1) * lanes]
        if adjoint:
            send_ref[rank, 0, 0] = kept_ref[rank, 0]
            send_ref[rank, 0, 1] = part
        else:
            send_ref[rank, 0] = part

    @pl.when(step_at == pl.num_programs(0) - 1)
    def _():
        for (start, stop), out_ref in zip(spans(given), out_refs):
            part = mixed_ref[start * mode_len : stop * mode_len]
            part = part.reshape(out_ref.shape[1:]).astype(jnp.bfloat16)
            for target in range(out_ref.shape[0]):
                out_ref[target] = part


def weight_kernel(terms_ref, spread_u_ref, spread_g_ref, out_ref):
    kx_len, step_len, row_len = out_ref.shape[:3]
    half = kx_len * row_len
    real_part, imag_part = 0.0, 0.0
    for sample in range(terms_ref.shape[0]):
        shape = (step_len, 2, half, CHANNELS * CHANNELS)
        spread_u = mode_rows(terms_ref[sample, 0, 0], spread_u_ref).reshape(shape)
        spread_g = mode_rows(terms_ref[sample, 0, 1], spread_g_ref).reshape(shape)
        u_real, u_imag = spread_u[:, 0], spread_u[:, 1]
        g_real, g_imag = spread_g[:, 0], spread_g[:, 1]
        real_part = real_part + (u_real * g_real + u_imag * g_imag)
        imag_part = imag_part + (u_real * g_imag - u_imag * g_real)
    for at in range(step_len):
        for kx in range(kx_len):
            rows = slice(kx * row_len, (kx + 1) * row_len)
            out_ref[kx, at, :, 0, :] = real_part[at, rows]
            out_ref[kx, at, :, 1, :] = imag_part[at, rows]


def whole_spec(array):
    zeros = (0,) * array.ndim
    return pl.BlockSpec(array.shape, lambda *at: zeros)


def params():
    return pltpu.CompilerParams(vmem_limit_bytes=VMEM_BYTES)


def cost(flops, bytes_accessed):
    return pl.CostEstimate(
        flops=int(flops), bytes_accessed=int(bytes_accessed), transcendentals=0
    )


def share_table(step_len, kx_len, row_len, share_len):
    ids = np.arange(step_len * 2 * kx_len * row_len)
    ids = ids.reshape(step_len * 2 * kx_len, row_len // share_len, share_len)
    ids = np.moveaxis(ids, 1, 0).reshape(-1)
    return (np.arange(ids.size)[:, None] == ids[None, :]).astype(ml_dtypes.bfloat16)


def shards(x_parts, y_parts, field, cotangent, spectral_weight):
    chan_len, x_len, y_len = field.shape[1:4]
    kx_len, mode_len, row_len = spectral_weight.shape[:3]
    parts = x_parts * y_parts
    dp_len = lax.axis_size("dp")
    share_len = row_len // dp_len
    step_len = min(4, mode_len)

    plane = plane_table(x_len, y_len, y_parts)
    back = jnp.asarray(plane.T.copy())
    plane = jnp.asarray(plane)
    forward_plain = jnp.asarray(analysis_table(np.ones(MZ)))
    forward_scaled = jnp.asarray(analysis_table(depth_scales()))
    back_scaled = jnp.asarray(synthesis_table(depth_scales()))
    back_plain = jnp.asarray(synthesis_table(np.ones(MZ)))
    cosines, sines = shift_tables(x_len, y_len, x_parts, y_parts)
    place = lax.axis_index("gx") * y_parts + lax.axis_index("gy")
    shift_cos = lax.dynamic_index_in_dim(jnp.asarray(cosines), place, 0, False)
    shift_sin = lax.dynamic_index_in_dim(jnp.asarray(sines), place, 0, False)

    pair_spec = pl.BlockSpec((parts, PAIR, mode_len, 128), lambda at: (0, at, 0, 0))
    grid_shape = jax.ShapeDtypeStruct((chan_len, x_len, y_len, NZ), jnp.bfloat16)
    grid_bytes = x_len * y_len * NZ * 2
    plane_flops = 2 * 2 * MX * MY * x_len * y_len * NZ * 2

    def spec_shape(size):
        return jax.ShapeDtypeStruct((parts, size, mode_len, 128), jnp.bfloat16)

    def pair_grid(start):
        return pl.BlockSpec(
            (PAIR, x_len, y_len, NZ), lambda at: (at + start // PAIR, 0, 0, 0)
        )

    def tables_of(*arrays):
        return [whole_spec(array) for array in arrays]

    def call(
        body, name, size, operands, specs, earlier, out_shapes, out_specs, scratch, flops, moved
    ):
        aliases = {}
        if earlier is not None:
            aliases = {len(operands): 0}
            operands = (*operands, earlier)
            specs = [*specs, pl.BlockSpec(memory_space=pl.ANY)]
        return pl.pallas_call(
            functools.partial(body, x_parts, y_parts),
            name=name,
            grid=(size // PAIR,),
            in_specs=specs,
            out_specs=out_specs,
            out_shape=out_shapes,
            scratch_shapes=scratch,
            input_output_aliases=aliases,
            compiler_params=params(),
            cost_estimate=cost(flops * size, moved * size),
        )(*operands)

    def mix(name, received, spread, gather, kept, taken, given):
        adjoint = kept is not None
        steps = mode_len // step_len
        lanes = step_len * 2 * kx_len * share_len
        small = (chan_len * mode_len, 128)
        operands = [*received, spectral_weight, spread, gather, share]
        specs = [
            *tables_of(*received),
            pl.BlockSpec(
                (kx_len, step_len, row_len, 2, chan_len * chan_len), lambda at: (0, at, 0, 0, 0)
            ),
            *tables_of(spread, gather, share),
        ]
        one_send = pl.BlockSpec((dp_len, 1, chan_len, lanes), lambda at: (0, at, 0, 0))
        if adjoint:
            operands.append(kept)
            specs.append(one_send)
            send_shape = (dp_len, steps, 2, chan_len, lanes)
            send_spec = pl.BlockSpec((dp_len, 1, 2, chan_len, lanes), lambda at: (0, at, 0, 0, 0))
        else:
            send_shape = (dp_len, steps, chan_len, lanes)
            send_spec = one_send
        whole = [spec_shape(size) for size in given]
        return pl.pallas_call(
            functools.partial(mix_kernel, adjoint, mode_len, step_len, taken, given),
            name=name,
            grid=(steps,),
            in_specs=specs,
            out_specs=[send_spec]
            + tables_of(*whole),
            out_shape=[jax.ShapeDtypeStruct(send_shape, jnp.float32)]
            + whole,
            scratch_shapes=[pltpu.VMEM(small, jnp.float32), pltpu.VMEM(small, jnp.float32)],
            compiler_params=params(),
            cost_estimate=cost(mode_len * 2e8, spectral_weight.size * 4),
        )(*operands)

    def exchange(blocks):
        return lax.all_to_all(blocks, ("gx", "gy"), 0, 0, tiled=True)

    share = jnp.asarray(share_table(step_len, kx_len, row_len, share_len))
    spread_in, spread_out = jnp.asarray(spread_input()), jnp.asarray(spread_output())
    onto_out = np.zeros((128, 128))
    onto_out[np.arange(128), np.arange(128) % CHANNELS] = 1.0
    onto_out = jnp.asarray(np.concatenate([onto_out, onto_out]).astype(ml_dtypes.bfloat16))
    onto_in = np.zeros((chan_len * chan_len, 128))
    onto_in[np.arange(chan_len * chan_len), np.arange(chan_len * chan_len) // CHANNELS] = 1.0
    onto_in = jnp.asarray(np.concatenate([onto_in, onto_in]).astype(ml_dtypes.bfloat16))

    received = []
    tables = (plane, forward_plain, shift_cos, shift_sin)
    for start, stop in spans(ANALYZE_CHUNKS):
        partial_u = call(
            analyze_kernel,
            "analyze_field",
            stop - start,
            (field[0], *tables),
            [pair_grid(start), *tables_of(*tables)],
            None,
            spec_shape(stop - start),
            pair_spec,
            [],
            plane_flops,
            grid_bytes,
        )
        received.append(exchange(partial_u))
    send_u, *spec_v = mix(
        "mix_forward", received, spread_in, onto_out, None, ANALYZE_CHUNKS, ACTIVATE_CHUNKS
    )

    received, out_grid = [], None
    gathered = [exchange(copies) for copies in spec_v]
    tables = (back, back_scaled, plane, forward_scaled, shift_cos, shift_sin)
    for chunk, (start, stop) in enumerate(spans(ACTIVATE_CHUNKS)):
        out_grid, partial_g = call(
            activate_kernel,
            "activate",
            stop - start,
            (gathered[chunk], cotangent[0], *tables),
            [pair_spec, pair_grid(start), *tables_of(*tables)],
            out_grid,
            [grid_shape, spec_shape(stop - start)],
            [pair_grid(start), pair_spec],
            [pltpu.VMEM((x_len * y_len, PAIR * NZ), jnp.bfloat16)],
            4 * plane_flops,
            2 * grid_bytes,
        )
        received.append(exchange(partial_g))
    send_terms, *spec_du = mix(
        "mix_adjoint", received, spread_out, onto_in, send_u, ACTIVATE_CHUNKS, SYNTHESIZE_CHUNKS
    )

    gathered = [exchange(copies) for copies in spec_du]
    terms = lax.all_to_all(send_terms, "dp", 0, 0, tiled=True)
    lanes = terms.shape[-1]
    weight_grad = pl.pallas_call(
        weight_kernel,
        name="weight_terms",
        grid=(mode_len // step_len,),
        in_specs=[
            pl.BlockSpec((dp_len, 1, 2, chan_len, lanes), lambda at: (0, at, 0, 0, 0)),
            *tables_of(spread_in, spread_out),
        ],
        out_specs=pl.BlockSpec(
            (kx_len, step_len, share_len, 2, chan_len * chan_len), lambda at: (0, at, 0, 0, 0)
        ),
        out_shape=jax.ShapeDtypeStruct(
            (kx_len, mode_len, share_len, 2, chan_len * chan_len), jnp.float32
        ),
        compiler_params=params(),
        cost_estimate=cost(mode_len * 2e8, mode_len * 2e6),
    )(terms, spread_in, spread_out)

    grad_grid = None
    tables = (back, back_plain, shift_cos, shift_sin)
    for chunk, (start, stop) in enumerate(spans(SYNTHESIZE_CHUNKS)):
        grad_grid = call(
            synthesize_kernel,
            "synthesize_grad",
            stop - start,
            (gathered[chunk], *tables),
            [pair_spec, *tables_of(*tables)],
            grad_grid,
            grid_shape,
            pair_grid(start),
            [],
            plane_flops,
            grid_bytes,
        )
    return (out_grid[None], grad_grid[None], weight_grad)


def solution(mesh):
    placed = (
        P("dp", None, "gx", "gy", None),
        P("dp", None, "gx", "gy", None),
        P("gy", "gx", None, None, None),
    )
    return jax.shard_map(
        functools.partial(shards, mesh.shape["gx"], mesh.shape["gy"]),
        mesh=mesh,
        in_specs=placed,
        out_specs=(
            P("dp", None, "gx", "gy", None),
            P("dp", None, "gx", "gy", None),
            P("gy", "gx", "dp", None, None),
        ),
        check_vma=False,
    )
```

```python
import functools
import math

import jax
import jax.numpy as jnp
import ml_dtypes
import numpy as np
from jax import lax
from jax.experimental import pallas as pl
from jax.experimental.pallas import tpu as pltpu
from jax.sharding import PartitionSpec as P

CHANNELS = 32
NX = 128
NY = 128
NZ = 128
MX = 16
MY = 16
MZ = 32
SAMPLES = 4
PAIR = 2
ANALYZE_CHUNKS = (16, 16)
ACTIVATE_CHUNKS = (16, 16)
SYNTHESIZE_CHUNKS = (16, 16)
PLANE_GAIN = 1.66526
VMEM_BYTES = 56 * 1024 * 1024

NN = (((1,), (0,)), ((), ()))


def f32_dot(left_op, right_op, dims=NN):
    return lax.dot_general(left_op, right_op, dims, preferred_element_type=jnp.float32)


def mode_list(length, count):
    half_ids = np.arange(count // 2)
    return np.concatenate([half_ids, length - count // 2 + half_ids])


def split_pair(table):
    high = table.astype(np.float32).astype(ml_dtypes.bfloat16)
    low = (table - high.astype(np.float64)).astype(np.float32).astype(ml_dtypes.bfloat16)
    return high, low


def depth_scales():
    return np.where(np.arange(MZ) == 0, 1.0, 2.0) / float(NX * NY * NZ)


def plane_angles(x_cells, y_cells, blocks):
    kx = mode_list(NX, MX)
    ky = mode_list(NY, MY)
    turns_x = (kx[:, None] * x_cells[None, :] % NX) / NX
    turns_y = (ky[:, None] * y_cells[None, :] % NY) / NY
    turns = turns_x[:, None, :, None] + turns_y[None, :, None, :]
    turns = turns.reshape(blocks, MX // blocks * MY, x_cells.size * y_cells.size)
    return 2.0 * math.pi * turns


def plane_table(x_len, y_len, blocks):
    angles = plane_angles(np.arange(x_len), np.arange(y_len), blocks)
    table = np.stack([np.cos(angles), -np.sin(angles)], axis=1)
    table = PLANE_GAIN * table.reshape(2 * MX * MY, x_len * y_len)
    return table.astype(np.float32).astype(ml_dtypes.bfloat16)


def plane_fit():
    exact = np.cos(2.0 * math.pi * np.arange(NX) / NX)
    rounded = (PLANE_GAIN * exact).astype(np.float32).astype(ml_dtypes.bfloat16)
    return (rounded.astype(np.float64) * exact).sum() / (exact * exact).sum()


def shift_tables(x_len, y_len, x_parts, y_parts):
    angles = plane_angles(np.arange(x_parts) * x_len, np.arange(y_parts) * y_len, y_parts)
    angles = np.moveaxis(angles, 2, 0)
    cosine = np.stack([np.cos(angles), np.cos(angles)], axis=2)
    signed = np.stack([np.sin(angles), -np.sin(angles)], axis=2)
    shape = (x_parts * y_parts, 1, 2 * MX * MY)
    cosine, signed = cosine / plane_fit(), signed / plane_fit()
    return cosine.reshape(shape).astype(np.float32), signed.reshape(shape).astype(np.float32)


def depth_angles():
    turns = (np.arange(MZ)[:, None] * np.arange(NZ)[None, :] % NZ) / NZ
    return 2.0 * math.pi * turns


def analysis_table(scale_vec):
    angles = depth_angles()
    table = np.concatenate([np.cos(angles), np.sin(angles)]) * np.tile(scale_vec, 2)[:, None]
    table = np.concatenate([table, table], axis=1).T
    blocks = np.kron(np.eye(PAIR), table)
    return blocks.astype(np.float32).astype(ml_dtypes.bfloat16)


def synthesis_table(scale_vec):
    angles = depth_angles()
    table = np.concatenate([np.cos(angles), np.sin(angles)]) * np.tile(scale_vec, 2)[:, None]
    high, low = split_pair(table.T)
    return np.concatenate([high, high, low], axis=1)


def spread_input():
    one = np.repeat(np.eye(CHANNELS), CHANNELS, axis=1)
    return np.concatenate([one, one]).astype(ml_dtypes.bfloat16)


def spread_output():
    one = np.tile(np.eye(CHANNELS), (1, CHANNELS))
    return np.concatenate([one, one]).astype(ml_dtypes.bfloat16)


def halves(value):
    high = value.astype(jnp.bfloat16)
    low = (value - high.astype(jnp.float32)).astype(jnp.bfloat16)
    return high, low


def swap_parts(value):
    width = value.shape[1]
    blocks = [
        pltpu.roll(value[:, at : at + 128], 64, 1) for at in range(0, width, 128)
    ]
    return jnp.concatenate(blocks, axis=1)


def part_signs(width):
    lane_ids = lax.broadcasted_iota(jnp.int32, (1, width), 1)
    return jnp.where(lane_ids % 128 < 64, 1.0, -1.0).astype(jnp.float32)


def analyze_pair(grids, plane_ref, depth_ref, cos_ref, sin_ref, out_ref, x_parts, y_parts):
    plane = f32_dot(plane_ref[...], grids)
    signs = part_signs(plane.shape[0])
    mode_len = MZ // x_parts
    sides = [half for chan in range(PAIR) for half in halves(plane[:, chan * NZ : (chan + 1) * NZ])]
    both = f32_dot(jnp.concatenate(sides, axis=1), depth_ref[...]).T
    for chan in range(PAIR):
        top = 2 * MZ * chan
        spectrum = both[top : top + MZ] + signs * swap_parts(both[top + MZ : top + 2 * MZ])
        spectrum = spectrum * cos_ref[...] + swap_parts(spectrum) * sin_ref[...]
        for gx in range(x_parts):
            for gy in range(y_parts):
                out_ref[gx * y_parts + gy, chan] = spectrum[
                    gx * mode_len : (gx + 1) * mode_len, gy * 128 : (gy + 1) * 128
                ].astype(jnp.bfloat16)


def depth_fields(spec_ref, depth_ref, cos_ref, sin_ref, x_parts, y_parts):
    fields = []
    for chan in range(PAIR):
        rows = [
            jnp.concatenate(
                [spec_ref[gx * y_parts + gy, chan].astype(jnp.float32) for gy in range(y_parts)],
                axis=1,
            )
            for gx in range(x_parts)
        ]
        spectrum = jnp.concatenate(rows, axis=0)
        spectrum = spectrum * cos_ref[...] - swap_parts(spectrum) * sin_ref[...]
        turned = -part_signs(spectrum.shape[1]) * swap_parts(spectrum)
        high, low = halves(jnp.concatenate([spectrum, turned], axis=0))
        fields.append(
            f32_dot(depth_ref[...], jnp.concatenate([high, low, high], axis=0)).T
        )
    return jnp.concatenate(fields, axis=1).astype(jnp.bfloat16)


def gelu_parts(pre_act):
    size = jnp.abs(pre_act)
    bell = jnp.exp(pre_act * pre_act * -0.5)
    turn = pl.reciprocal(1.0 + (0.3275911 * 0.7071067811865476) * size, approx=False)
    poly = 0.5 * 1.061405429 * turn - 0.5 * 1.453152027
    poly = poly * turn + 0.5 * 1.421413741
    poly = poly * turn - 0.5 * 0.284496736
    poly = poly * turn + 0.5 * 0.254829592
    tail = poly * turn * bell
    value = jnp.maximum(pre_act, 0.0) - size * tail
    normal_cdf = jnp.where(pre_act > 0.0, 1.0 - tail, tail)
    return value, normal_cdf + pre_act * bell * 0.3989422804014327


def analyze_kernel(x_parts, y_parts, grid_ref, plane_ref, depth_ref, cos_ref, sin_ref, out_ref):
    cells = grid_ref.shape[1] * grid_ref.shape[2]
    grids = jnp.concatenate(
        [grid_ref[chan].reshape(cells, NZ) for chan in range(PAIR)], axis=1
    )
    analyze_pair(grids, plane_ref, depth_ref, cos_ref, sin_ref, out_ref, x_parts, y_parts)


def activate_kernel(
    x_parts,
    y_parts,
    spec_ref,
    cot_ref,
    back_ref,
    back_depth_ref,
    plane_ref,
    depth_ref,
    cos_ref,
    sin_ref,
    *rest,
):
    value_ref, out_ref, grad_ref = rest[-3:]
    fields = depth_fields(spec_ref, back_depth_ref, cos_ref, sin_ref, x_parts, y_parts)
    x_len, y_len = cot_ref.shape[1], cot_ref.shape[2]
    step = min(8, x_len)
    for x_at in range(0, x_len, step):
        rows = slice(x_at * y_len, (x_at + step) * y_len)
        pre_act = f32_dot(back_ref[rows], fields)
        for chan in range(PAIR):
            lanes = slice(chan * NZ, (chan + 1) * NZ)
            value, slope = gelu_parts(pre_act[:, lanes])
            value_ref[chan, x_at : x_at + step] = value.astype(jnp.bfloat16).reshape(step, y_len, NZ)
            cotangent = cot_ref[chan, x_at : x_at + step].reshape(step * y_len, NZ)
            grad_ref[rows, lanes] = (cotangent.astype(jnp.float32) * slope).astype(jnp.bfloat16)
    analyze_pair(
        grad_ref[...], plane_ref, depth_ref, cos_ref, sin_ref, out_ref, x_parts, y_parts
    )


def synthesize_kernel(
    x_parts, y_parts, spec_ref, back_ref, depth_ref, cos_ref, sin_ref, *rest
):
    out_ref = rest[-1]
    fields = depth_fields(spec_ref, depth_ref, cos_ref, sin_ref, x_parts, y_parts)
    x_len, y_len = out_ref.shape[1], out_ref.shape[2]
    step = min(8, x_len)
    for x_at in range(0, x_len, step):
        rows = slice(x_at * y_len, (x_at + step) * y_len)
        grid = f32_dot(back_ref[rows], fields)
        for chan in range(PAIR):
            out_ref[chan, x_at : x_at + step] = (
                grid[:, chan * NZ : (chan + 1) * NZ].astype(jnp.bfloat16).reshape(step, y_len, NZ)
            )


def mode_rows(value, spread_ref):
    high = value.astype(jnp.bfloat16).astype(jnp.float32)
    both = jnp.concatenate([high, value - high], axis=0)
    return f32_dot(both.T.astype(jnp.bfloat16), spread_ref[...])


def spans(chunks):
    ends = np.cumsum(chunks)
    return [(int(end) - size, int(end)) for size, end in zip(chunks, ends)]


def mix_kernel(adjoint, mode_len, step_len, taken, given, *refs):
    recv_refs, refs = refs[: len(taken)], refs[len(taken) :]
    weight_ref, spread_ref, gather_ref, share_ref, *refs = refs
    send_ref, *out_refs, taken_ref, mixed_ref = refs
    step_at = pl.program_id(0)

    @pl.when(step_at == 0)
    def _():
        for (start, stop), recv_ref in zip(spans(taken), recv_refs):
            total = recv_ref[0].astype(jnp.float32)
            for source in range(1, recv_ref.shape[0]):
                total = total + recv_ref[source].astype(jnp.float32)
            rows = slice(start * mode_len, stop * mode_len)
            taken_ref[rows] = total.reshape((stop - start) * mode_len, 128)

    half = 64
    inputs = []
    for at in range(step_len):
        mode_at = step_at * step_len + at
        here = pl.ds(mode_at, CHANNELS, stride=mode_len) if mode_len > 1 else slice(None)
        inputs.append(taken_ref[here, :])
        spread = mode_rows(inputs[-1], spread_ref)
        real_in, imag_in = spread[:half], spread[half:]
        w_real = weight_ref[:, at, :, 0, :].reshape(half, CHANNELS * CHANNELS)
        w_imag = weight_ref[:, at, :, 1, :].reshape(half, CHANNELS * CHANNELS)
        if adjoint:
            real_part = real_in * w_real + imag_in * w_imag
            imag_part = imag_in * w_real - real_in * w_imag
            terms = jnp.concatenate([real_part, imag_part], axis=0)
        else:
            real_part = real_in * w_real - imag_in * w_imag
            imag_part = imag_in * w_real + real_in * w_imag
            terms = jnp.concatenate([real_part, imag_part], axis=0)
            width = terms.shape[1]
            while width > 128:
                width //= 2
                terms = terms[:, :width] + terms[:, width:]
        high, low = halves(terms)
        mixed = f32_dot(jnp.concatenate([high, low], axis=1), gather_ref[...])
        mixed_ref[here, :] = mixed.T[:CHANNELS]

    high, low = halves(jnp.concatenate(inputs, axis=1))
    shared = f32_dot(jnp.concatenate([high, low], axis=0), share_ref[...])
    shared = shared[:CHANNELS] + shared[CHANNELS:]
    lanes = send_ref.shape[-1]
    for rank in range(send_ref.shape[0]):
        send_ref[rank, 0] = shared[:, rank * lanes : (rank + 1) * lanes]

    @pl.when(step_at == pl.num_programs(0) - 1)
    def _():
        for (start, stop), out_ref in zip(spans(given), out_refs):
            part = mixed_ref[start * mode_len : stop * mode_len]
            part = part.reshape(out_ref.shape[1:]).astype(jnp.bfloat16)
            for target in range(out_ref.shape[0]):
                out_ref[target] = part


def weight_kernel(rank_ref, u_ref, g_ref, spread_u_ref, spread_g_ref, out_ref):
    kx_len, step_len, row_len = out_ref.shape[:3]
    half = kx_len * row_len
    real_part, imag_part = 0.0, 0.0
    for sample in range(u_ref.shape[0]):
        shape = (step_len, 2, half, CHANNELS * CHANNELS)
        spread_u = mode_rows(u_ref[sample, 0, 0], spread_u_ref).reshape(shape)
        spread_g = mode_rows(g_ref[sample, 0, 0], spread_g_ref).reshape(shape)
        u_real, u_imag = spread_u[:, 0], spread_u[:, 1]
        g_real, g_imag = spread_g[:, 0], spread_g[:, 1]
        real_part = real_part + (u_real * g_real + u_imag * g_imag)
        imag_part = imag_part + (u_real * g_imag - u_imag * g_real)
    for at in range(step_len):
        for kx in range(kx_len):
            rows = slice(kx * row_len, (kx + 1) * row_len)
            out_ref[kx, at, :, 0, :] = real_part[at, rows]
            out_ref[kx, at, :, 1, :] = imag_part[at, rows]


def whole_spec(array):
    zeros = (0,) * array.ndim
    return pl.BlockSpec(array.shape, lambda *at: zeros)


def params():
    return pltpu.CompilerParams(vmem_limit_bytes=VMEM_BYTES)


def cost(flops, bytes_accessed):
    return pl.CostEstimate(
        flops=int(flops), bytes_accessed=int(bytes_accessed), transcendentals=0
    )


def share_table(step_len, kx_len, row_len, share_len):
    ids = np.arange(step_len * 2 * kx_len * row_len)
    ids = ids.reshape(step_len * 2 * kx_len, row_len // share_len, share_len)
    ids = np.moveaxis(ids, 1, 0).reshape(-1)
    return (np.arange(ids.size)[:, None] == ids[None, :]).astype(ml_dtypes.bfloat16)


def shards(x_parts, y_parts, field, cotangent, spectral_weight):
    chan_len, x_len, y_len = field.shape[1:4]
    kx_len, mode_len, row_len = spectral_weight.shape[:3]
    parts = x_parts * y_parts
    dp_len = lax.axis_size("dp")
    share_len = row_len // dp_len
    step_len = min(4, mode_len)

    plane = plane_table(x_len, y_len, y_parts)
    back = jnp.asarray(plane.T.copy())
    plane = jnp.asarray(plane)
    forward_plain = jnp.asarray(analysis_table(np.ones(MZ)))
    forward_scaled = jnp.asarray(analysis_table(depth_scales()))
    back_scaled = jnp.asarray(synthesis_table(depth_scales()))
    back_plain = jnp.asarray(synthesis_table(np.ones(MZ)))
    cosines, sines = shift_tables(x_len, y_len, x_parts, y_parts)
    place = lax.axis_index("gx") * y_parts + lax.axis_index("gy")
    shift_cos = lax.dynamic_index_in_dim(jnp.asarray(cosines), place, 0, False)
    shift_sin = lax.dynamic_index_in_dim(jnp.asarray(sines), place, 0, False)

    pair_spec = pl.BlockSpec((parts, PAIR, mode_len, 128), lambda at: (0, at, 0, 0))
    grid_shape = jax.ShapeDtypeStruct((chan_len, x_len, y_len, NZ), jnp.bfloat16)
    grid_bytes = x_len * y_len * NZ * 2
    plane_flops = 2 * 2 * MX * MY * x_len * y_len * NZ * 2

    def spec_shape(size):
        return jax.ShapeDtypeStruct((parts, size, mode_len, 128), jnp.bfloat16)

    def pair_grid(start):
        return pl.BlockSpec(
            (PAIR, x_len, y_len, NZ), lambda at: (at + start // PAIR, 0, 0, 0)
        )

    def tables_of(*arrays):
        return [whole_spec(array) for array in arrays]

    def call(
        body, name, size, operands, specs, earlier, out_shapes, out_specs, scratch, flops, moved
    ):
        aliases = {}
        if earlier is not None:
            aliases = {len(operands): 0}
            operands = (*operands, earlier)
            specs = [*specs, pl.BlockSpec(memory_space=pl.ANY)]
        return pl.pallas_call(
            functools.partial(body, x_parts, y_parts),
            name=name,
            grid=(size // PAIR,),
            in_specs=specs,
            out_specs=out_specs,
            out_shape=out_shapes,
            scratch_shapes=scratch,
            input_output_aliases=aliases,
            compiler_params=params(),
            cost_estimate=cost(flops * size, moved * size),
        )(*operands)

    def mix(name, received, spread, gather, adjoint, taken, given):
        steps = mode_len // step_len
        lanes = step_len * 2 * kx_len * share_len
        small = (chan_len * mode_len, 128)
        operands = [*received, spectral_weight, spread, gather, share]
        specs = [
            *tables_of(*received),
            pl.BlockSpec(
                (kx_len, step_len, row_len, 2, chan_len * chan_len), lambda at: (0, at, 0, 0, 0)
            ),
            *tables_of(spread, gather, share),
        ]
        send_shape = (dp_len, steps, chan_len, lanes)
        send_spec = pl.BlockSpec((dp_len, 1, chan_len, lanes), lambda at: (0, at, 0, 0))
        whole = [spec_shape(size) for size in given]
        return pl.pallas_call(
            functools.partial(mix_kernel, adjoint, mode_len, step_len, taken, given),
            name=name,
            grid=(steps,),
            in_specs=specs,
            out_specs=[send_spec]
            + tables_of(*whole),
            out_shape=[jax.ShapeDtypeStruct(send_shape, jnp.float32)]
            + whole,
            scratch_shapes=[pltpu.VMEM(small, jnp.float32), pltpu.VMEM(small, jnp.float32)],
            compiler_params=params(),
            cost_estimate=cost(mode_len * 2e8, spectral_weight.size * 4),
        )(*operands)

    def exchange(blocks):
        return lax.all_to_all(blocks, ("gx", "gy"), 0, 0, tiled=True)

    share = jnp.asarray(share_table(step_len, kx_len, row_len, share_len))
    spread_in, spread_out = jnp.asarray(spread_input()), jnp.asarray(spread_output())
    onto_out = np.zeros((128, 128))
    onto_out[np.arange(128), np.arange(128) % CHANNELS] = 1.0
    onto_out = jnp.asarray(np.concatenate([onto_out, onto_out]).astype(ml_dtypes.bfloat16))
    onto_in = np.zeros((chan_len * chan_len, 128))
    onto_in[np.arange(chan_len * chan_len), np.arange(chan_len * chan_len) // CHANNELS] = 1.0
    onto_in = jnp.asarray(np.concatenate([onto_in, onto_in]).astype(ml_dtypes.bfloat16))

    received = []
    tables = (plane, forward_plain, shift_cos, shift_sin)
    for start, stop in spans(ANALYZE_CHUNKS):
        partial_u = call(
            analyze_kernel,
            "analyze_field",
            stop - start,
            (field[0], *tables),
            [pair_grid(start), *tables_of(*tables)],
            None,
            spec_shape(stop - start),
            pair_spec,
            [],
            plane_flops,
            grid_bytes,
        )
        received.append(exchange(partial_u))
    send_u, *spec_v = mix(
        "mix_forward", received, spread_in, onto_out, False, ANALYZE_CHUNKS, ACTIVATE_CHUNKS
    )

    all_u = lax.all_gather(send_u, "dp", axis=0, tiled=False)
    received, out_grid = [], None
    gathered = [exchange(copies) for copies in spec_v]
    tables = (back, back_scaled, plane, forward_scaled, shift_cos, shift_sin)
    for chunk, (start, stop) in enumerate(spans(ACTIVATE_CHUNKS)):
        out_grid, partial_g = call(
            activate_kernel,
            "activate",
            stop - start,
            (gathered[chunk], cotangent[0], *tables),
            [pair_spec, pair_grid(start), *tables_of(*tables)],
            out_grid,
            [grid_shape, spec_shape(stop - start)],
            [pair_grid(start), pair_spec],
            [pltpu.VMEM((x_len * y_len, PAIR * NZ), jnp.bfloat16)],
            4 * plane_flops,
            2 * grid_bytes,
        )
        received.append(exchange(partial_g))
    send_g, *spec_du = mix(
        "mix_adjoint", received, spread_out, onto_in, True, ACTIVATE_CHUNKS, SYNTHESIZE_CHUNKS
    )

    gathered = [exchange(copies) for copies in spec_du]
    all_g = lax.all_gather(send_g, "dp", axis=0, tiled=False)
    lanes = all_g.shape[-1]
    terms_spec = pl.BlockSpec(
        (dp_len, 1, 1, chan_len, lanes), lambda at, rank: (0, rank[0], at, 0, 0)
    )
    weight_grad = pl.pallas_call(
        weight_kernel,
        name="weight_terms",
        grid_spec=pltpu.PrefetchScalarGridSpec(
            num_scalar_prefetch=1,
            grid=(mode_len // step_len,),
            in_specs=[terms_spec, terms_spec, *tables_of(spread_in, spread_out)],
            out_specs=pl.BlockSpec(
                (kx_len, step_len, share_len, 2, chan_len * chan_len),
                lambda at, rank: (0, at, 0, 0, 0),
            ),
        ),
        out_shape=jax.ShapeDtypeStruct(
            (kx_len, mode_len, share_len, 2, chan_len * chan_len), jnp.float32
        ),
        compiler_params=params(),
        cost_estimate=cost(mode_len * 2e8, mode_len * 2e6),
    )(lax.axis_index("dp").astype(jnp.int32).reshape(1), all_u, all_g, spread_in, spread_out)

    grad_grid = None
    tables = (back, back_plain, shift_cos, shift_sin)
    for chunk, (start, stop) in enumerate(spans(SYNTHESIZE_CHUNKS)):
        grad_grid = call(
            synthesize_kernel,
            "synthesize_grad",
            stop - start,
            (gathered[chunk], *tables),
            [pair_spec, *tables_of(*tables)],
            grad_grid,
            grid_shape,
            pair_grid(start),
            [],
            plane_flops,
            grid_bytes,
        )
    return (out_grid[None], grad_grid[None], weight_grad)


def solution(mesh):
    placed = (
        P("dp", None, "gx", "gy", None),
        P("dp", None, "gx", "gy", None),
        P("gy", "gx", None, None, None),
    )
    return jax.shard_map(
        functools.partial(shards, mesh.shape["gx"], mesh.shape["gy"]),
        mesh=mesh,
        in_specs=placed,
        out_specs=(
            P("dp", None, "gx", "gy", None),
            P("dp", None, "gx", "gy", None),
            P("gy", "gx", "dp", None, None),
        ),
        check_vma=False,
    )
```

```python
import functools
import math

import jax
import jax.numpy as jnp
import ml_dtypes
import numpy as np
from jax import lax
from jax.experimental import pallas as pl
from jax.experimental.pallas import tpu as pltpu
from jax.sharding import PartitionSpec as P

CHANNELS = 32
NX = 128
NY = 128
NZ = 128
MX = 16
MY = 16
MZ = 32
SAMPLES = 4
PAIR = 2
ANALYZE_CHUNKS = (16, 16)
ACTIVATE_CHUNKS = (16, 16)
SYNTHESIZE_CHUNKS = (16, 16)
PLANE_GAIN = 1.66526
VMEM_BYTES = 56 * 1024 * 1024

NN = (((1,), (0,)), ((), ()))
NT = (((1,), (1,)), ((), ()))


def f32_dot(left_op, right_op, dims=NN):
    return lax.dot_general(left_op, right_op, dims, preferred_element_type=jnp.float32)


def mode_list(length, count):
    half_ids = np.arange(count // 2)
    return np.concatenate([half_ids, length - count // 2 + half_ids])


def split_pair(table):
    high = table.astype(np.float32).astype(ml_dtypes.bfloat16)
    low = (table - high.astype(np.float64)).astype(np.float32).astype(ml_dtypes.bfloat16)
    return high, low


def depth_scales():
    return np.where(np.arange(MZ) == 0, 1.0, 2.0) / float(NX * NY * NZ)


def plane_angles(x_cells, y_cells, blocks):
    kx = mode_list(NX, MX)
    ky = mode_list(NY, MY)
    turns_x = (kx[:, None] * x_cells[None, :] % NX) / NX
    turns_y = (ky[:, None] * y_cells[None, :] % NY) / NY
    turns = turns_x[:, None, :, None] + turns_y[None, :, None, :]
    turns = turns.reshape(blocks, MX // blocks * MY, x_cells.size * y_cells.size)
    return 2.0 * math.pi * turns


def plane_table(x_len, y_len, blocks):
    angles = plane_angles(np.arange(x_len), np.arange(y_len), blocks)
    table = np.stack([np.cos(angles), -np.sin(angles)], axis=1)
    table = PLANE_GAIN * table.reshape(2 * MX * MY, x_len * y_len)
    return table.astype(np.float32).astype(ml_dtypes.bfloat16)


def plane_fit():
    exact = np.cos(2.0 * math.pi * np.arange(NX) / NX)
    rounded = (PLANE_GAIN * exact).astype(np.float32).astype(ml_dtypes.bfloat16)
    return (rounded.astype(np.float64) * exact).sum() / (exact * exact).sum()


def shift_tables(x_len, y_len, x_parts, y_parts):
    angles = plane_angles(np.arange(x_parts) * x_len, np.arange(y_parts) * y_len, y_parts)
    angles = np.moveaxis(angles, 2, 0)
    cosine = np.stack([np.cos(angles), np.cos(angles)], axis=2)
    signed = np.stack([np.sin(angles), -np.sin(angles)], axis=2)
    shape = (x_parts * y_parts, 1, 2 * MX * MY)
    cosine, signed = cosine / plane_fit(), signed / plane_fit()
    return cosine.reshape(shape).astype(np.float32), signed.reshape(shape).astype(np.float32)


def depth_angles():
    turns = (np.arange(MZ)[:, None] * np.arange(NZ)[None, :] % NZ) / NZ
    return 2.0 * math.pi * turns


def analysis_table(scale_vec):
    angles = depth_angles()
    table = np.concatenate([np.cos(angles), np.sin(angles)]) * np.tile(scale_vec, 2)[:, None]
    table = table.astype(np.float32).astype(ml_dtypes.bfloat16)
    return np.concatenate([table, table], axis=1)


def synthesis_table(scale_vec):
    angles = depth_angles()
    table = np.concatenate([np.cos(angles), np.sin(angles)]) * np.tile(scale_vec, 2)[:, None]
    high, low = split_pair(table.T)
    return np.concatenate([high, high, low], axis=1)


def spread_input():
    one = np.repeat(np.eye(CHANNELS), CHANNELS, axis=1)
    return np.concatenate([one, one]).astype(ml_dtypes.bfloat16)


def spread_output():
    one = np.tile(np.eye(CHANNELS), (1, CHANNELS))
    return np.concatenate([one, one]).astype(ml_dtypes.bfloat16)


def halves(value):
    high = value.astype(jnp.bfloat16)
    low = (value - high.astype(jnp.float32)).astype(jnp.bfloat16)
    return high, low


def swap_parts(value):
    width = value.shape[1]
    blocks = [
        pltpu.roll(value[:, at : at + 128], 64, 1) for at in range(0, width, 128)
    ]
    return jnp.concatenate(blocks, axis=1)


def part_signs(width):
    lane_ids = lax.broadcasted_iota(jnp.int32, (1, width), 1)
    return jnp.where(lane_ids % 128 < 64, 1.0, -1.0).astype(jnp.float32)


def finish_pair(plane, depth_ref, cos_ref, sin_ref, out_ref, first, x_parts, y_parts):
    signs = part_signs(plane.shape[0])
    mode_len = MZ // x_parts
    for chan in range(PAIR):
        sides = jnp.concatenate(halves(plane[:, chan * NZ : (chan + 1) * NZ]), axis=1)
        both = f32_dot(depth_ref[...], sides, NT)
        spectrum = both[:MZ] + signs * swap_parts(both[MZ:])
        spectrum = spectrum * cos_ref[...] + swap_parts(spectrum) * sin_ref[...]
        for gx in range(x_parts):
            for gy in range(y_parts):
                out_ref[gx * y_parts + gy, first + chan] = spectrum[
                    gx * mode_len : (gx + 1) * mode_len, gy * 128 : (gy + 1) * 128
                ].astype(jnp.bfloat16)


def depth_fields(spec_ref, depth_ref, cos_ref, sin_ref, x_parts, y_parts, first=0):
    fields = []
    for chan in range(first, first + PAIR):
        rows = [
            jnp.concatenate(
                [spec_ref[gx * y_parts + gy, chan].astype(jnp.float32) for gy in range(y_parts)],
                axis=1,
            )
            for gx in range(x_parts)
        ]
        spectrum = jnp.concatenate(rows, axis=0)
        spectrum = spectrum * cos_ref[...] - swap_parts(spectrum) * sin_ref[...]
        turned = -part_signs(spectrum.shape[1]) * swap_parts(spectrum)
        high, low = halves(jnp.concatenate([spectrum, turned], axis=0))
        fields.append(
            f32_dot(depth_ref[...], jnp.concatenate([high, low, high], axis=0)).astype(jnp.bfloat16)
        )
    return jnp.concatenate(fields, axis=0)


def gelu_parts(pre_act):
    size = jnp.abs(pre_act)
    bell = jnp.exp(pre_act * pre_act * -0.5)
    turn = pl.reciprocal(1.0 + (0.3275911 * 0.7071067811865476) * size, approx=False)
    poly = 0.5 * 1.061405429 * turn - 0.5 * 1.453152027
    poly = poly * turn + 0.5 * 1.421413741
    poly = poly * turn - 0.5 * 0.284496736
    poly = poly * turn + 0.5 * 0.254829592
    tail = poly * turn * bell
    value = jnp.maximum(pre_act, 0.0) - size * tail
    normal_cdf = jnp.where(pre_act > 0.0, 1.0 - tail, tail)
    return value, normal_cdf + pre_act * bell * 0.3989422804014327


def lagged(steps, first, second):
    step_at = pl.program_id(0)

    @pl.when(step_at == 0)
    def _():
        first(step_at, None)

    @pl.when((step_at > 0) & (step_at < steps))
    def _():
        first(step_at, second)

    @pl.when(step_at == steps)
    def _():
        second(step_at - 1)


def analyze_kernel(
    x_parts, y_parts, grid_ref, plane_ref, depth_ref, cos_ref, sin_ref, out_ref, sums_ref
):
    cells = grid_ref.shape[1] * grid_ref.shape[2]

    def second(step_at):
        finish_pair(
            sums_ref[...], depth_ref, cos_ref, sin_ref, out_ref, step_at * PAIR, x_parts, y_parts
        )

    def first(step_at, earlier):
        if earlier is not None:
            earlier(step_at - 1)
        grids = [grid_ref[chan].reshape(cells, NZ) for chan in range(PAIR)]
        sums_ref[...] = f32_dot(plane_ref[...], jnp.concatenate(grids, axis=1))

    lagged(pl.num_programs(0) - 1, first, second)


def activate_kernel(
    x_parts,
    y_parts,
    spec_ref,
    cot_ref,
    back_ref,
    back_depth_ref,
    plane_ref,
    depth_ref,
    cos_ref,
    sin_ref,
    *rest,
):
    value_ref, out_ref, early_ref, late_ref = rest[-4:]
    x_len, y_len = cot_ref.shape[1], cot_ref.shape[2]
    block = min(16, x_len)
    step = min(8, x_len)

    def activate(fields, new_ref, chan_at, x_at):
        rows = slice(x_at * y_len, (x_at + step) * y_len)
        pre_act = f32_dot(back_ref[rows], fields, NT)
        for chan in range(PAIR):
            lanes = slice(chan * NZ, (chan + 1) * NZ)
            value, slope = gelu_parts(pre_act[:, lanes])
            here = (chan_at + chan, slice(x_at, x_at + step))
            value_ref[here] = value.astype(jnp.bfloat16).reshape(step, y_len, NZ)
            cotangent = cot_ref[here].reshape(step * y_len, NZ).astype(jnp.float32)
            new_ref[rows, lanes] = (cotangent * slope).astype(jnp.bfloat16)

    def stage(fields, new_ref, chan_at, old_ref, old_first):
        sums = None
        for x_at in range(0, x_len, block):
            if old_ref is not None:
                rows = slice(x_at * y_len, (x_at + block) * y_len)
                part = f32_dot(plane_ref[:, rows], old_ref[rows])
                sums = part if sums is None else sums + part
            if fields is not None:
                for at in range(x_at, x_at + block, step):
                    activate(fields, new_ref, chan_at, at)
        if old_ref is not None:
            finish_pair(
                sums, depth_ref, cos_ref, sin_ref, out_ref, old_first, x_parts, y_parts
            )

    def second(step_at):
        stage(None, None, None, late_ref, (2 * step_at + 1) * PAIR)

    def first(step_at, earlier):
        fields = [
            depth_fields(spec_ref, back_depth_ref, cos_ref, sin_ref, x_parts, y_parts, first)
            for first in (0, PAIR)
        ]
        if earlier is None:
            stage(fields[0], early_ref, 0, None, None)
        else:
            stage(fields[0], early_ref, 0, late_ref, (2 * step_at - 1) * PAIR)
        stage(fields[1], late_ref, PAIR, early_ref, 2 * step_at * PAIR)

    lagged(pl.num_programs(0) - 1, first, second)


def synthesize_kernel(
    x_parts, y_parts, spec_ref, back_ref, depth_ref, cos_ref, sin_ref, *rest
):
    out_ref, fields_ref = rest[-2:]
    x_len, y_len = out_ref.shape[1], out_ref.shape[2]
    step = min(8, x_len)

    def second(step_at):
        for x_at in range(0, x_len, step):
            rows = slice(x_at * y_len, (x_at + step) * y_len)
            grid = f32_dot(back_ref[rows], fields_ref[...], NT)
            for chan in range(PAIR):
                out_ref[chan, x_at : x_at + step] = (
                    grid[:, chan * NZ : (chan + 1) * NZ]
                    .astype(jnp.bfloat16)
                    .reshape(step, y_len, NZ)
                )

    def first(step_at, earlier):
        fields = depth_fields(spec_ref, depth_ref, cos_ref, sin_ref, x_parts, y_parts)
        if earlier is not None:
            earlier(step_at - 1)
        fields_ref[...] = fields

    lagged(pl.num_programs(0) - 1, first, second)


def mode_rows(value, spread_ref):
    high = value.astype(jnp.bfloat16).astype(jnp.float32)
    both = jnp.concatenate([high, value - high], axis=0)
    return f32_dot(both.T.astype(jnp.bfloat16), spread_ref[...])


def spans(chunks):
    ends = np.cumsum(chunks)
    return [(int(end) - size, int(end)) for size, end in zip(chunks, ends)]


def mix_kernel(adjoint, mode_len, step_len, taken, given, *refs):
    recv_refs, refs = refs[: len(taken)], refs[len(taken) :]
    weight_ref, spread_ref, gather_ref, share_ref, *refs = refs
    send_ref, *out_refs, taken_ref, mixed_ref = refs
    step_at = pl.program_id(0)

    @pl.when(step_at == 0)
    def _():
        for (start, stop), recv_ref in zip(spans(taken), recv_refs):
            total = recv_ref[0].astype(jnp.float32)
            for source in range(1, recv_ref.shape[0]):
                total = total + recv_ref[source].astype(jnp.float32)
            rows = slice(start * mode_len, stop * mode_len)
            taken_ref[rows] = total.reshape((stop - start) * mode_len, 128)

    half = 64
    inputs = []
    for at in range(step_len):
        mode_at = step_at * step_len + at
        here = pl.ds(mode_at, CHANNELS, stride=mode_len) if mode_len > 1 else slice(None)
        inputs.append(taken_ref[here, :])
        spread = mode_rows(inputs[-1], spread_ref)
        real_in, imag_in = spread[:half], spread[half:]
        w_real = weight_ref[:, at, :, 0, :].reshape(half, CHANNELS * CHANNELS)
        w_imag = weight_ref[:, at, :, 1, :].reshape(half, CHANNELS * CHANNELS)
        if adjoint:
            real_part = real_in * w_real + imag_in * w_imag
            imag_part = imag_in * w_real - real_in * w_imag
            terms = jnp.concatenate([real_part, imag_part], axis=0)
        else:
            real_part = real_in * w_real - imag_in * w_imag
            imag_part = imag_in * w_real + real_in * w_imag
            terms = jnp.concatenate([real_part, imag_part], axis=0)
            width = terms.shape[1]
            while width > 128:
                width //= 2
                terms = terms[:, :width] + terms[:, width:]
        high, low = halves(terms)
        mixed = f32_dot(jnp.concatenate([high, low], axis=1), gather_ref[...])
        mixed_ref[here, :] = mixed.T[:CHANNELS]

    high, low = halves(jnp.concatenate(inputs, axis=1))
    shared = f32_dot(jnp.concatenate([high, low], axis=0), share_ref[...])
    shared = shared[:CHANNELS] + shared[CHANNELS:]
    lanes = send_ref.shape[-1]
    for rank in range(send_ref.shape[0]):
        send_ref[rank, 0] = shared[:, rank * lanes : (rank + 1) * lanes]

    @pl.when(step_at == pl.num_programs(0) - 1)
    def _():
        for (start, stop), out_ref in zip(spans(given), out_refs):
            part = mixed_ref[start * mode_len : stop * mode_len]
            part = part.reshape(out_ref.shape[1:]).astype(jnp.bfloat16)
            for target in range(out_ref.shape[0]):
                out_ref[target] = part


def weight_kernel(rank_ref, u_ref, g_ref, spread_u_ref, spread_g_ref, out_ref):
    kx_len, step_len, row_len = out_ref.shape[:3]
    half = kx_len * row_len
    real_part, imag_part = 0.0, 0.0
    for sample in range(u_ref.shape[0]):
        shape = (step_len, 2, half, CHANNELS * CHANNELS)
        spread_u = mode_rows(u_ref[sample, 0, 0], spread_u_ref).reshape(shape)
        spread_g = mode_rows(g_ref[sample, 0, 0], spread_g_ref).reshape(shape)
        u_real, u_imag = spread_u[:, 0], spread_u[:, 1]
        g_real, g_imag = spread_g[:, 0], spread_g[:, 1]
        real_part = real_part + (u_real * g_real + u_imag * g_imag)
        imag_part = imag_part + (u_real * g_imag - u_imag * g_real)
    for at in range(step_len):
        for kx in range(kx_len):
            rows = slice(kx * row_len, (kx + 1) * row_len)
            out_ref[kx, at, :, 0, :] = real_part[at, rows]
            out_ref[kx, at, :, 1, :] = imag_part[at, rows]


def whole_spec(array):
    zeros = (0,) * array.ndim
    return pl.BlockSpec(array.shape, lambda *at: zeros)


def params():
    return pltpu.CompilerParams(vmem_limit_bytes=VMEM_BYTES)


def cost(flops, bytes_accessed):
    return pl.CostEstimate(
        flops=int(flops), bytes_accessed=int(bytes_accessed), transcendentals=0
    )


def share_table(step_len, kx_len, row_len, share_len):
    ids = np.arange(step_len * 2 * kx_len * row_len)
    ids = ids.reshape(step_len * 2 * kx_len, row_len // share_len, share_len)
    ids = np.moveaxis(ids, 1, 0).reshape(-1)
    return (np.arange(ids.size)[:, None] == ids[None, :]).astype(ml_dtypes.bfloat16)


def shards(x_parts, y_parts, field, cotangent, spectral_weight):
    chan_len, x_len, y_len = field.shape[1:4]
    kx_len, mode_len, row_len = spectral_weight.shape[:3]
    parts = x_parts * y_parts
    dp_len = lax.axis_size("dp")
    share_len = row_len // dp_len
    step_len = min(4, mode_len)

    plane = plane_table(x_len, y_len, y_parts)
    back = jnp.asarray(plane.T.copy())
    plane = jnp.asarray(plane)
    forward_plain = jnp.asarray(analysis_table(np.ones(MZ)))
    forward_scaled = jnp.asarray(analysis_table(depth_scales()))
    back_scaled = jnp.asarray(synthesis_table(depth_scales()))
    back_plain = jnp.asarray(synthesis_table(np.ones(MZ)))
    cosines, sines = shift_tables(x_len, y_len, x_parts, y_parts)
    place = lax.axis_index("gx") * y_parts + lax.axis_index("gy")
    shift_cos = lax.dynamic_index_in_dim(jnp.asarray(cosines), place, 0, False)
    shift_sin = lax.dynamic_index_in_dim(jnp.asarray(sines), place, 0, False)

    grid_shape = jax.ShapeDtypeStruct((chan_len, x_len, y_len, NZ), jnp.bfloat16)
    grid_bytes = x_len * y_len * NZ * 2
    plane_flops = 2 * 2 * MX * MY * x_len * y_len * NZ * 2

    def spec_shape(size):
        return jax.ShapeDtypeStruct((parts, size, mode_len, 128), jnp.bfloat16)

    def spec_blocks(size, width):
        last = size // width - 1
        return pl.BlockSpec(
            (parts, width, mode_len, 128), lambda at: (0, jnp.minimum(at, last), 0, 0)
        )

    def grid_blocks(start, size, width, lag=0):
        last = size // width - 1
        return pl.BlockSpec(
            (width, x_len, y_len, NZ),
            lambda at: (jnp.clip(at - lag, 0, last) + start // width, 0, 0, 0),
        )

    def tables_of(*arrays):
        return [whole_spec(array) for array in arrays]

    def call(
        body, name, size, width, operands, specs, earlier, out_shapes, out_specs, scratch, flops, moved
    ):
        aliases = {}
        if earlier is not None:
            aliases = {len(operands): 0}
            operands = (*operands, earlier)
            specs = [*specs, pl.BlockSpec(memory_space=pl.ANY)]
        return pl.pallas_call(
            functools.partial(body, x_parts, y_parts),
            name=name,
            grid=(size // width + 1,),
            in_specs=specs,
            out_specs=out_specs,
            out_shape=out_shapes,
            scratch_shapes=scratch,
            input_output_aliases=aliases,
            compiler_params=params(),
            cost_estimate=cost(flops * size, moved * size),
        )(*operands)

    def mix(name, received, spread, gather, adjoint, taken, given):
        steps = mode_len // step_len
        lanes = step_len * 2 * kx_len * share_len
        small = (chan_len * mode_len, 128)
        operands = [*received, spectral_weight, spread, gather, share]
        specs = [
            *tables_of(*received),
            pl.BlockSpec(
                (kx_len, step_len, row_len, 2, chan_len * chan_len), lambda at: (0, at, 0, 0, 0)
            ),
            *tables_of(spread, gather, share),
        ]
        send_shape = (dp_len, steps, chan_len, lanes)
        send_spec = pl.BlockSpec((dp_len, 1, chan_len, lanes), lambda at: (0, at, 0, 0))
        whole = [spec_shape(size) for size in given]
        return pl.pallas_call(
            functools.partial(mix_kernel, adjoint, mode_len, step_len, taken, given),
            name=name,
            grid=(steps,),
            in_specs=specs,
            out_specs=[send_spec]
            + tables_of(*whole),
            out_shape=[jax.ShapeDtypeStruct(send_shape, jnp.float32)]
            + whole,
            scratch_shapes=[pltpu.VMEM(small, jnp.float32), pltpu.VMEM(small, jnp.float32)],
            compiler_params=params(),
            cost_estimate=cost(mode_len * 2e8, spectral_weight.size * 4),
        )(*operands)

    def exchange(blocks):
        return lax.all_to_all(blocks, ("gx", "gy"), 0, 0, tiled=True)

    share = jnp.asarray(share_table(step_len, kx_len, row_len, share_len))
    spread_in, spread_out = jnp.asarray(spread_input()), jnp.asarray(spread_output())
    onto_out = np.zeros((128, 128))
    onto_out[np.arange(128), np.arange(128) % CHANNELS] = 1.0
    onto_out = jnp.asarray(np.concatenate([onto_out, onto_out]).astype(ml_dtypes.bfloat16))
    onto_in = np.zeros((chan_len * chan_len, 128))
    onto_in[np.arange(chan_len * chan_len), np.arange(chan_len * chan_len) // CHANNELS] = 1.0
    onto_in = jnp.asarray(np.concatenate([onto_in, onto_in]).astype(ml_dtypes.bfloat16))

    received = []
    tables = (plane, forward_plain, shift_cos, shift_sin)
    for start, stop in spans(ANALYZE_CHUNKS):
        partial_u = call(
            analyze_kernel,
            "analyze_field",
            stop - start,
            PAIR,
            (field[0], *tables),
            [grid_blocks(start, stop - start, PAIR), *tables_of(*tables)],
            None,
            spec_shape(stop - start),
            whole_spec(spec_shape(stop - start)),
            [pltpu.VMEM((2 * MX * MY, PAIR * NZ), jnp.float32)],
            plane_flops,
            grid_bytes,
        )
        received.append(exchange(partial_u))
    send_u, *spec_v = mix(
        "mix_forward", received, spread_in, onto_out, False, ANALYZE_CHUNKS, ACTIVATE_CHUNKS
    )

    all_u = lax.all_gather(send_u, "dp", axis=0, tiled=False)
    received, out_grid = [], None
    gathered = [exchange(copies) for copies in spec_v]
    tables = (back, back_scaled, plane, forward_scaled, shift_cos, shift_sin)
    for chunk, (start, stop) in enumerate(spans(ACTIVATE_CHUNKS)):
        out_grid, partial_g = call(
            activate_kernel,
            "activate",
            stop - start,
            2 * PAIR,
            (gathered[chunk], cotangent[0], *tables),
            [
                spec_blocks(stop - start, 2 * PAIR),
                grid_blocks(start, stop - start, 2 * PAIR),
                *tables_of(*tables),
            ],
            out_grid,
            [grid_shape, spec_shape(stop - start)],
            [grid_blocks(start, stop - start, 2 * PAIR), whole_spec(spec_shape(stop - start))],
            [pltpu.VMEM((x_len * y_len, PAIR * NZ), jnp.bfloat16) for _ in range(2)],
            4 * plane_flops,
            2 * grid_bytes,
        )
        received.append(exchange(partial_g))
    send_g, *spec_du = mix(
        "mix_adjoint", received, spread_out, onto_in, True, ACTIVATE_CHUNKS, SYNTHESIZE_CHUNKS
    )

    gathered = [exchange(copies) for copies in spec_du]
    all_g = lax.all_gather(send_g, "dp", axis=0, tiled=False)
    lanes = all_g.shape[-1]
    terms_spec = pl.BlockSpec(
        (dp_len, 1, 1, chan_len, lanes), lambda at, rank: (0, rank[0], at, 0, 0)
    )
    weight_grad = pl.pallas_call(
        weight_kernel,
        name="weight_terms",
        grid_spec=pltpu.PrefetchScalarGridSpec(
            num_scalar_prefetch=1,
            grid=(mode_len // step_len,),
            in_specs=[terms_spec, terms_spec, *tables_of(spread_in, spread_out)],
            out_specs=pl.BlockSpec(
                (kx_len, step_len, share_len, 2, chan_len * chan_len),
                lambda at, rank: (0, at, 0, 0, 0),
            ),
        ),
        out_shape=jax.ShapeDtypeStruct(
            (kx_len, mode_len, share_len, 2, chan_len * chan_len), jnp.float32
        ),
        compiler_params=params(),
        cost_estimate=cost(mode_len * 2e8, mode_len * 2e6),
    )(lax.axis_index("dp").astype(jnp.int32).reshape(1), all_u, all_g, spread_in, spread_out)

    grad_grid = None
    tables = (back, back_plain, shift_cos, shift_sin)
    for chunk, (start, stop) in enumerate(spans(SYNTHESIZE_CHUNKS)):
        grad_grid = call(
            synthesize_kernel,
            "synthesize_grad",
            stop - start,
            PAIR,
            (gathered[chunk], *tables),
            [spec_blocks(stop - start, PAIR), *tables_of(*tables)],
            grad_grid,
            grid_shape,
            grid_blocks(start, stop - start, PAIR, 1),
            [pltpu.VMEM((PAIR * NZ, 2 * MX * MY), jnp.bfloat16)],
            plane_flops,
            grid_bytes,
        )
    return (out_grid[None], grad_grid[None], weight_grad)


def solution(mesh):
    placed = (
        P("dp", None, "gx", "gy", None),
        P("dp", None, "gx", "gy", None),
        P("gy", "gx", None, None, None),
    )
    return jax.shard_map(
        functools.partial(shards, mesh.shape["gx"], mesh.shape["gy"]),
        mesh=mesh,
        in_specs=placed,
        out_specs=(
            P("dp", None, "gx", "gy", None),
            P("dp", None, "gx", "gy", None),
            P("gy", "gx", "dp", None, None),
        ),
        check_vma=False,
    )
```
